512 devices in a mesh: patch: 32 (over x, y_hi, core), section: 8 (over z), cfg: 2 (over y_lo).
Axes of the slice: x: 4, y: 8 (y_hi: 4, y_lo: 2; y = y_hi * 2 + y_lo), z: 8, core: 2. Of those that a mesh axis runs over, the one named last changes fastest.
Arguments:
- hidden: bfloat16 [2, 512, 1536], P('cfg', 'patch'), may hold values from -6 to 6
- timestep: int32 [1], replicated, may hold values from 0 to 27
- patch_order: int32 [64], replicated, may hold values from 0 to 63, each once
- modulation: float32 [8, 2, 28, 4608], P('section', 'cfg'), may hold values from -4 to 4
- qkv_weight: bfloat16 [8, 1536, 4608], P('section', None, 'patch'), may hold values from -0.15625 to 0.15625
- stale_kv: bfloat16 [8, 2, 512, 3072], P('section', 'cfg', 'patch'), may hold values from -6 to 6
Outputs:
- guided: bfloat16 [512, 1536], P(('patch', 'section'), 'cfg')
- fresh_kv: bfloat16 [8, 2, 512, 3072], P('section', 'cfg', 'patch')
The draws below stay inside these ranges and needn't reach their ends.
Inputs may be any that keep to these rules, and one draw needn't show every extreme that they name: `patch_order`: each patch appears once.
All inputs are finite; a program needn't handle non-finite values.
Results may differ from the reference program's by a relative error of at most 0.023.
Values may be sent and summed in bfloat16 or wider, within the bound.
No kernel may reach another device: no remote copies, remote signals or barrier semaphores. Data moves between devices by JAX's collectives and lax.ppermute only.
A program may use at most 64 MiB of HBM per device.

```python
import math
import jax
import jax.numpy as jnp
from jax import lax

HEADS = 12
HDIM = 128
STEPS = 28
ROWS = 8
D = 1536
PATCHES = 64
TOKENS = 512
N_SECTION = 8
N_CFG = 2


def levels(key, dims, shards, low, top_value):
    level = 1.0
    for position, shards_of in shards:
        heights = jax.random.uniform(jax.random.fold_in(jax.random.fold_in(key, 6), position), (shards_of,), jnp.float32, low / len(shards), top_value / len(shards))
        level = level * jnp.repeat(jnp.exp(heights), dims[position] // shards_of).reshape((-1,) + (1,) * (len(dims) - 1 - position))
    return level


def noise(own_key, shape, deviation, bound, cuts=(), kind=jnp.bfloat16):
    result = deviation * jax.random.normal(own_key, shape, jnp.float32)
    if cuts:
        result = result * levels(own_key, shape, cuts, -0.22, 0.18)
    return jnp.clip(result, -bound, bound).astype(kind)


def setup_inputs(seed: int = 0) -> dict:
    key_list = jax.random.split(jax.random.key(seed), 7)
    hidden = noise(key_list[0], (N_CFG, TOKENS, D), 1.0, 6.0, ((0, 2), (1, 32)))
    timestep = jax.random.randint(key_list[1], (1,), 0, STEPS).astype(jnp.int32)
    patch_order = jax.random.permutation(key_list[2], PATCHES).astype(jnp.int32)
    modulation = noise(key_list[3], (N_SECTION, N_CFG, STEPS, 3 * D), 1.0, 4.0, ((0, 8), (1, 2)), jnp.float32)
    qkv_weight = noise(key_list[4], (N_SECTION, D, 3 * D), D ** -0.5, 0.15625, ((0, 8), (2, 32)))
    stale_kv = noise(key_list[5], (N_SECTION, N_CFG, TOKENS, 2 * D), 1.0, 6.0, ((0, 8), (1, 2), (2, 32)))
    return dict(hidden=hidden, timestep=timestep, patch_order=patch_order, modulation=modulation, qkv_weight=qkv_weight, stale_kv=stale_kv)


guide_weight = 3.5
norm_eps = 1e-06

def stored(values):
    return lax.optimization_barrier(values.astype(jnp.bfloat16))

def head_norm(values):
    shaped = values.astype(jnp.float32).reshape(values.shape[0], HEADS, HDIM)
    return shaped * lax.rsqrt(lax.optimization_barrier(jnp.mean(shaped * shaped, axis=-1, keepdims=True)) + norm_eps)

def rotate(shaped, positions):
    halfway = HDIM // 2
    inverse = jnp.exp(-math.log(10000.0) * jnp.arange(halfway, dtype=jnp.float32) / halfway)
    angles = positions.astype(jnp.float32)[:, None] * inverse[None, :]
    cosine = jnp.cos(angles)[:, None, :]
    sine_part = jnp.sin(angles)[:, None, :]
    first_half = shaped[..., :halfway]
    second = shaped[..., halfway:]
    return jnp.concatenate([first_half * cosine - second * sine_part, first_half * sine_part + second * cosine], axis=-1)

def section_block(states, table, weight, stale_rows, timestep, positions):
    feat_width = HEADS * HDIM
    table_row = lax.dynamic_index_in_dim(table, timestep[0], 0, keepdims=False)
    shifts = table_row[:feat_width]
    scales = table_row[feat_width:2 * feat_width]
    gate_vector = table_row[2 * feat_width:]
    values32 = states.astype(jnp.float32)
    center = lax.optimization_barrier(jnp.mean(values32, axis=-1, keepdims=True))
    spread = lax.optimization_barrier(jnp.mean((values32 - center) ** 2, axis=-1, keepdims=True))
    normed = stored((values32 - center) * lax.rsqrt(spread + norm_eps) * (1.0 + scales) + shifts)
    projected = stored(jnp.dot(normed, weight, preferred_element_type=jnp.float32))
    queries = stored(rotate(head_norm(projected[:, :feat_width]), positions))
    fresh_keys = stored(rotate(head_norm(projected[:, feat_width:2 * feat_width]), positions))
    fresh_values = projected[:, 2 * feat_width:]
    stale_keys = stale_rows[:, :feat_width].astype(jnp.float32).reshape(TOKENS, HEADS, HDIM)
    stale_values = stale_rows[:, feat_width:].astype(jnp.float32).reshape(TOKENS, HEADS, HDIM)
    query_f = queries.astype(jnp.float32)
    key_f = fresh_keys.astype(jnp.float32)
    value_f = fresh_values.astype(jnp.float32).reshape(TOKENS, HEADS, HDIM)
    scale_factor = 1.0 / math.sqrt(HDIM)
    columns = jnp.arange(TOKENS, dtype=jnp.int32) // ROWS

    def attend(block_index):
        offset = (block_index * ROWS).astype(jnp.int32)
        query_blk = lax.dynamic_slice_in_dim(query_f, offset, ROWS, 0)
        key_blk = lax.dynamic_slice_in_dim(key_f, offset, ROWS, 0)
        value_blk = lax.dynamic_slice_in_dim(value_f, offset, ROWS, 0)
        scores = jnp.einsum('rhd,thd->hrt', query_blk, stale_keys) * scale_factor
        weights = jnp.where((columns == block_index)[None, None, :], 0.0, jnp.exp(scores))
        own_weights = jnp.exp(jnp.einsum('rhd,thd->hrt', query_blk, key_blk) * scale_factor)
        denominator = lax.optimization_barrier(jnp.sum(weights, axis=-1)) + lax.optimization_barrier(jnp.sum(own_weights, axis=-1))
        numerator = jnp.einsum('hrt,thd->rhd', stored(weights).astype(jnp.float32), stale_values)
        numerator = numerator + jnp.einsum('hrt,thd->rhd', stored(own_weights).astype(jnp.float32), value_blk)
        return (numerator / jnp.transpose(denominator)[:, :, None]).reshape(ROWS, feat_width)
    attended = lax.map(attend, jnp.arange(PATCHES, dtype=jnp.int32)).reshape(TOKENS, feat_width)
    new_states = stored(values32 + gate_vector * attended)
    fresh = jnp.concatenate([fresh_keys.reshape(TOKENS, feat_width), fresh_values], axis=1)
    return (new_states, fresh)

def reference(hidden, timestep, patch_order, modulation, qkv_weight, stale_kv):
    positions = (patch_order[:, None] * ROWS + jnp.arange(ROWS, dtype=jnp.int32)[None, :]).reshape(TOKENS).astype(jnp.int32)
    finals = []
    caches = []
    for branch in range(2):
        states = hidden[branch]
        per_section = []
        for section_num in range(N_SECTION):
            states, fresh = section_block(states, modulation[section_num, branch], qkv_weight[section_num], stale_kv[section_num, branch], timestep, positions)
            per_section.append(fresh)
        finals.append(states.astype(jnp.float32))
        caches.append(jnp.stack(per_section))
    guided = stored(finals[0] + guide_weight * (finals[1] - finals[0]))
    fresh_kv = jnp.stack(caches, axis=1)
    return (guided, fresh_kv)
```

```python
import functools
import math

import jax
import jax.numpy as jnp
import numpy as np
from jax import lax
from jax.experimental import pallas as pl
from jax.experimental.pallas import tpu as pltpu
from jax.sharding import Mesh, PartitionSpec as P

HEADS = 12
HDIM = 128
ROWS = 8
D = HEADS * HDIM
TOKENS = 512
SECTIONS = 8
MEMBERS = 4
PART = D // MEMBERS
LOCAL = 16
GROUP = LOCAL * MEMBERS
RING = 16
UNIT = 24
SHARE = 3 * UNIT

guide_weight = 3.5
norm_eps = 1e-06

AXES = ("xh", "xl", "yh", "core", "section", "cfg")
SIZES = (2, 2, 4, 2, 8, 2)


def ring_place(place):
    return (0, place) if place < 8 else (1, 15 - place)


def plan_weight_moves():
    def plane(xh, xl, y, core):
        return (((xh * 2 + xl) * 4 + y // 2) * 2 + core) * 2 + y % 2

    left = [[] for _ in range(64)]
    for unit in range(3 * D // UNIT):
        source, slot = divmod(unit, 3)
        part, within = divmod(unit, D // UNIT)
        member, within = divmod(within, PART // UNIT)
        place, target_slot = divmod(part * (PART // UNIT) + within, 3)
        xh, y = ring_place(place)
        target = plane(xh, member // 2, y, member % 2)
        left[source].append((target, slot, target_slot))
    rounds = []
    for _ in range(3):
        owner = {}

        def place_edge(source, seen):
            for edge in sorted(left[source], key=lambda e: e[0] != source):
                if edge[0] in seen:
                    continue
                seen.add(edge[0])
                if edge[0] not in owner or place_edge(owner[edge[0]][0], seen):
                    owner[edge[0]] = (source, edge)
                    return True
            return False

        for source in range(64):
            if not place_edge(source, set()):
                raise ValueError("no matching")
        for source, edge in owner.values():
            left[source].remove(edge)
        rounds.append([(source, edge) for source, edge in owner.values()])
    routes, send_slot, take = [], np.zeros((3, 64), np.int32), np.zeros((3, 64), np.int32)
    for number, matched in enumerate(rounds):
        route = []
        for source, (target, slot, target_slot) in matched:
            send_slot[number, source] = slot
            take[target_slot, target] = number
            for s in range(SECTIONS):
                route.append(((source // 2 * 8 + s) * 2 + source % 2, (target // 2 * 8 + s) * 2 + target % 2))
        routes.append(route)
    return routes, send_slot, take


ROUTES, SEND_SLOT, TAKE = plan_weight_moves()
RING_GROUPS = [[xh * 8 + y for xh, y in map(ring_place, range(RING))]]
PAIRS = (
    [[s, s + 1] for s in range(0, SECTIONS, 2)],
    [[s, (s + 1) % SECTIONS] for s in range(1, SECTIONS, 2)],
)


def nt_dot(a, b):
    return lax.dot_general(a, b, (((1,), (1,)), ((), ())), preferred_element_type=jnp.float32)


def block_kernel(tick, who, x_ref, w_ref, kv_ref, mod_ref, gate_ref, cos_ref, sin_ref, block_ref, old_ref, state_ref, fresh_ref):
    member = who[0]
    active = who[1] == tick
    xs = [x_ref[i].astype(jnp.float32) for i in range(MEMBERS)]
    center = sum(jnp.sum(x, axis=-1, keepdims=True) for x in xs) / D
    xs = [x - center for x in xs]
    spread = sum(jnp.sum(x * x, axis=-1, keepdims=True) for x in xs) / D
    inv = lax.rsqrt(spread + norm_eps)
    normed = jnp.concatenate(
        [
            (
                xs[i] * inv * (1.0 + mod_ref[1:2, i * PART : (i + 1) * PART])
                + mod_ref[0:1, i * PART : (i + 1) * PART]
            ).astype(jnp.bfloat16)
            for i in range(MEMBERS)
        ],
        axis=1,
    )
    projected = nt_dot(normed, w_ref[...]).astype(jnp.bfloat16)
    row_block = block_ref[...]
    stale_mask = lax.broadcasted_iota(jnp.int32, (GROUP, TOKENS), 1) // ROWS == row_block
    own_mask = (
        lax.broadcasted_iota(jnp.int32, (GROUP, GROUP), 0) // ROWS
        == lax.broadcasted_iota(jnp.int32, (GROUP, GROUP), 1) // ROWS
    )
    cosine, sine = cos_ref[...], sin_ref[...]

    def turned(values):
        values = values.astype(jnp.float32)
        values = values * lax.rsqrt(jnp.mean(values * values, axis=-1, keepdims=True) + norm_eps)
        return (values * cosine + pltpu.roll(values, HDIM // 2, 1) * sine).astype(jnp.bfloat16)

    scale = 1.0 / math.sqrt(HDIM)
    for head in range(PART // HDIM):
        cols = slice(head * HDIM, (head + 1) * HDIM)
        query = turned(projected[:, head * HDIM : (head + 1) * HDIM])
        key = turned(projected[:, PART + head * HDIM : PART + (head + 1) * HDIM])
        value = projected[:, 2 * PART + head * HDIM : 2 * PART + (head + 1) * HDIM]
        weights = jnp.where(stale_mask, 0.0, jnp.exp(nt_dot(query, kv_ref[:, cols]) * scale))
        own = jnp.where(own_mask, jnp.exp(nt_dot(query, key) * scale), 0.0)
        total = jnp.sum(weights, axis=-1, keepdims=True) + jnp.sum(own, axis=-1, keepdims=True)
        attended = jnp.dot(
            weights.astype(jnp.bfloat16),
            kv_ref[:, PART + head * HDIM : PART + (head + 1) * HDIM],
            preferred_element_type=jnp.float32,
        ) + jnp.dot(own.astype(jnp.bfloat16), value, preferred_element_type=jnp.float32)
        attended = attended / total
        state = x_ref[member, :, cols].astype(jnp.float32) + gate_ref[0:1, cols] * attended
        state_ref[:, cols] = state.astype(jnp.bfloat16)
        fresh_ref[:, cols] = jnp.where(active, key, old_ref[:, cols])
        vcols = slice(PART + head * HDIM, PART + (head + 1) * HDIM)
        fresh_ref[:, vcols] = jnp.where(active, value, old_ref[:, vcols])


def run_block(tick, who, x, weight, kv, mod, gate, cosine, sine, blocks, old):
    vmem = pl.BlockSpec(memory_space=pltpu.VMEM)
    return pl.pallas_call(
        functools.partial(block_kernel, tick),
        out_shape=(
            jax.ShapeDtypeStruct((GROUP, PART), jnp.bfloat16),
            jax.ShapeDtypeStruct((GROUP, 2 * PART), jnp.bfloat16),
        ),
        in_specs=[pl.BlockSpec(memory_space=pltpu.SMEM)] + [vmem] * 9,
        out_specs=(vmem, vmem),
        compiler_params=pltpu.CompilerParams(vmem_limit_bytes=24 * 1024 * 1024),
        name="block_step",
    )(who, x, weight, kv, mod, gate, cosine, sine, blocks, old)


def body(hidden, timestep, patch_order, modulation, qkv_weight, stale_kv):
    index = {a: lax.axis_index(a) for a in AXES}
    section = index["section"]
    member = index["xl"] * 2 + index["core"]
    place = (((index["xh"] * 2 + index["xl"]) * 4 + index["yh"]) * 2 + index["core"]) * 2 + index["cfg"]

    columns = jnp.transpose(qkv_weight[0])
    half = lax.dynamic_slice_in_dim(columns, index["cfg"] * SHARE, SHARE, 0).reshape(3, UNIT, D)
    moved = []
    for number in range(3):
        slot = jnp.asarray(SEND_SLOT[number])[place]
        moved.append(lax.ppermute(lax.dynamic_index_in_dim(half, slot, 0, keepdims=False), AXES, ROUTES[number]))
    moved = jnp.stack(moved)
    share = jnp.concatenate(
        [lax.dynamic_index_in_dim(moved, jnp.asarray(TAKE[j])[place], 0, keepdims=False) for j in range(3)]
    )
    weight = lax.all_gather(share, ("xh", "yh", "cfg"), axis=0, tiled=True, axis_index_groups=RING_GROUPS)

    share, stale_rows, entering = lax.optimization_barrier((share, stale_kv[0, 0], hidden[0]))
    pieces = [
        jnp.concatenate(
            [stale_rows[:, m * PART : (m + 1) * PART], stale_rows[:, D + m * PART : D + (m + 1) * PART]], axis=1
        )
        for m in range(MEMBERS)
    ]
    outgoing = jnp.stack([pieces[(p // 8 % 2) * 2 + p % 2] for p in range(32)])
    kv = lax.all_to_all(outgoing, ("xh", "xl", "yh", "core"), split_axis=0, concat_axis=0, tiled=True)
    kv = kv.reshape(TOKENS, 2 * PART)

    x = lax.all_gather(entering, ("xl", "core"), axis=0, tiled=True)
    x = jnp.transpose(x.reshape(GROUP, MEMBERS, PART), (1, 0, 2))

    row = lax.dynamic_index_in_dim(modulation[0, 0], timestep[0], 0, keepdims=False)
    mod = row[: 2 * D].reshape(2, D)
    gate = lax.dynamic_slice_in_dim(row, 2 * D + member * PART, PART, 0).reshape(1, PART)

    lane = jnp.arange(GROUP, dtype=jnp.int32)
    source = lane // LOCAL
    patch = ((index["xh"] * 2 + source // 2) * 4 + index["yh"]) * 2 + source % 2
    blocks = patch * (LOCAL // ROWS) + lane % LOCAL // ROWS
    positions = (patch_order[blocks] * ROWS + lane % ROWS).astype(jnp.float32)
    halfway = HDIM // 2
    inverse = jnp.exp(-math.log(10000.0) * jnp.arange(halfway, dtype=jnp.float32) / halfway)
    angles = positions[:, None] * inverse[None, :]
    cosine, sine = jnp.cos(angles), jnp.sin(angles)
    cosine = jnp.concatenate([cosine, cosine], axis=1)
    sine = jnp.concatenate([-sine, sine], axis=1)

    who = jnp.stack([member, section]).astype(jnp.int32)
    fresh = jnp.zeros((GROUP, 2 * PART), jnp.bfloat16)
    for tick in range(SECTIONS):
        state, fresh = run_block(tick, who, x, weight, kv, mod, gate, cosine, sine, blocks[:, None], fresh)
        if tick + 1 < SECTIONS:
            state = lax.all_gather(state, "section", axis=0, tiled=False, axis_index_groups=PAIRS[tick % 2])[0]
            x = lax.all_gather(state, ("xl", "core"), axis=0, tiled=False)

    ends = lax.all_gather(jnp.concatenate([state, fresh], axis=1), ("xl", "core"), axis=0, tiled=False)
    ends = lax.dynamic_slice_in_dim(ends, member * LOCAL, LOCAL, 1)
    ends = jnp.transpose(ends, (1, 0, 2))
    finals = ends[:, :, :PART].reshape(SECTIONS, LOCAL // SECTIONS, 2, D // 2)
    fresh_all = jnp.concatenate(
        [ends[:, :, PART : 2 * PART].reshape(LOCAL, D), ends[:, :, 2 * PART :].reshape(LOCAL, D)], axis=1
    )
    finals = jnp.transpose(finals, (0, 2, 1, 3)).reshape(SECTIONS * 2, LOCAL // SECTIONS, D // 2)
    spread = lax.all_to_all(finals, ("section", "cfg"), split_axis=0, concat_axis=0, tiled=True)
    uncond = spread[2 * SECTIONS - 2].astype(jnp.float32)
    conditioned = spread[2 * SECTIONS - 1].astype(jnp.float32)
    guided = (uncond + guide_weight * (conditioned - uncond)).astype(jnp.bfloat16)
    return guided, fresh_all[None, None]


def solution(mesh):
    fine = Mesh(mesh.devices.reshape(SIZES), AXES)
    patch = ("xh", "xl", "yh", "core")
    return jax.shard_map(
        body,
        mesh=fine,
        in_specs=(
            P("cfg", patch, None),
            P(),
            P(),
            P("section", "cfg", None, None),
            P("section", None, patch),
            P("section", "cfg", patch, None),
        ),
        out_specs=(P((*patch, "section"), "cfg"), P("section", "cfg", patch, None)),
        check_vma=False,
    )
```

```python
import functools
import math

import jax
import jax.numpy as jnp
import numpy as np
from jax import lax
from jax.experimental import pallas as pl
from jax.experimental.pallas import tpu as pltpu
from jax.sharding import Mesh, PartitionSpec as P

HEADS = 12
HDIM = 128
ROWS = 8
D = HEADS * HDIM
TOKENS = 512
SECTIONS = 8
MEMBERS = 4
PART = D // MEMBERS
LOCAL = 16
GROUP = LOCAL * MEMBERS
UNIT = 24
SHARE = 3 * UNIT

guide_weight = 3.5
norm_eps = 1e-06

AXES = ("xh", "xl", "yh", "core", "section", "cfg")
SIZES = (2, 2, 4, 2, 8, 2)


def plan_weight_moves():
    def plane(xh, xl, y, core):
        return (((xh * 2 + xl) * 4 + y // 2) * 2 + core) * 2 + y % 2

    left = [[] for _ in range(64)]
    for unit in range(3 * D // UNIT):
        source, slot = divmod(unit, 3)
        part, within = divmod(unit, D // UNIT)
        member, within = divmod(within, PART // UNIT)
        place, target_slot = divmod(part * (PART // UNIT) + within, 3)
        y, xh = divmod(place, 2)
        target = plane(xh, member // 2, y, member % 2)
        left[source].append((target, slot, target_slot))
    rounds = []
    for _ in range(3):
        owner = {}

        def place_edge(source, seen):
            for edge in sorted(left[source], key=lambda e: e[0] != source):
                if edge[0] in seen:
                    continue
                seen.add(edge[0])
                if edge[0] not in owner or place_edge(owner[edge[0]][0], seen):
                    owner[edge[0]] = (source, edge)
                    return True
            return False

        for source in range(64):
            if not place_edge(source, set()):
                raise ValueError("no matching")
        for source, edge in owner.values():
            left[source].remove(edge)
        rounds.append([(source, edge) for source, edge in owner.values()])
    routes, send_slot, take = [], np.zeros((3, 64), np.int32), np.zeros((3, 64), np.int32)
    for number, matched in enumerate(rounds):
        route = []
        for source, (target, slot, target_slot) in matched:
            send_slot[number, source] = slot
            take[target_slot, target] = number
            for s in range(SECTIONS):
                route.append(((source // 2 * 8 + s) * 2 + source % 2, (target // 2 * 8 + s) * 2 + target % 2))
        routes.append(route)
    return routes, send_slot, take


ROUTES, SEND_SLOT, TAKE = plan_weight_moves()
SLOTS = np.concatenate([SEND_SLOT.reshape(-1), TAKE.reshape(-1)])
PAIRS = (
    [[s, s + 1] for s in range(0, SECTIONS, 2)],
    [[s, (s + 1) % SECTIONS] for s in range(1, SECTIONS, 2)],
)


def nt_dot(a, b):
    return lax.dot_general(a, b, (((1,), (1,)), ((), ())), preferred_element_type=jnp.float32)


def block_kernel(tick, who, x_ref, w_ref, kv_ref, mod_ref, gate_ref, cos_ref, sin_ref, block_ref, old_ref, state_ref, fresh_ref):
    member = who[0]
    active = who[1] == tick
    xs = [x_ref[i].astype(jnp.float32) for i in range(MEMBERS)]
    center = sum(jnp.sum(x, axis=-1, keepdims=True) for x in xs) / D
    xs = [x - center for x in xs]
    spread = sum(jnp.sum(x * x, axis=-1, keepdims=True) for x in xs) / D
    inv = lax.rsqrt(spread + norm_eps)
    normed = jnp.concatenate(
        [
            (
                xs[i] * inv * (1.0 + mod_ref[1:2, i * PART : (i + 1) * PART])
                + mod_ref[0:1, i * PART : (i + 1) * PART]
            ).astype(jnp.bfloat16)
            for i in range(MEMBERS)
        ],
        axis=1,
    )
    projected = nt_dot(normed, w_ref[...]).astype(jnp.bfloat16)
    row_block = block_ref[...]
    stale_mask = lax.broadcasted_iota(jnp.int32, (GROUP, TOKENS), 1) // ROWS == row_block
    own_mask = (
        lax.broadcasted_iota(jnp.int32, (GROUP, GROUP), 0) // ROWS
        == lax.broadcasted_iota(jnp.int32, (GROUP, GROUP), 1) // ROWS
    )
    cosine, sine = cos_ref[...], sin_ref[...]

    def turned(values):
        values = values.astype(jnp.float32)
        values = values * lax.rsqrt(jnp.mean(values * values, axis=-1, keepdims=True) + norm_eps)
        return (values * cosine + pltpu.roll(values, HDIM // 2, 1) * sine).astype(jnp.bfloat16)

    scale = 1.0 / math.sqrt(HDIM)
    for head in range(PART // HDIM):
        cols = slice(head * HDIM, (head + 1) * HDIM)
        query = turned(projected[:, head * HDIM : (head + 1) * HDIM])
        key = turned(projected[:, PART + head * HDIM : PART + (head + 1) * HDIM])
        value = projected[:, 2 * PART + head * HDIM : 2 * PART + (head + 1) * HDIM]
        weights = jnp.where(stale_mask, 0.0, jnp.exp(nt_dot(query, kv_ref[:, cols]) * scale))
        own = jnp.where(own_mask, jnp.exp(nt_dot(query, key) * scale), 0.0)
        total = jnp.sum(weights, axis=-1, keepdims=True) + jnp.sum(own, axis=-1, keepdims=True)
        attended = jnp.dot(
            weights.astype(jnp.bfloat16),
            kv_ref[:, PART + head * HDIM : PART + (head + 1) * HDIM],
            preferred_element_type=jnp.float32,
        ) + jnp.dot(own.astype(jnp.bfloat16), value, preferred_element_type=jnp.float32)
        attended = attended / total
        state = x_ref[member, :, cols].astype(jnp.float32) + gate_ref[0:1, cols] * attended
        state_ref[:, cols] = state.astype(jnp.bfloat16)
        fresh_ref[:, cols] = jnp.where(active, key, old_ref[:, cols])
        vcols = slice(PART + head * HDIM, PART + (head + 1) * HDIM)
        fresh_ref[:, vcols] = jnp.where(active, value, old_ref[:, vcols])


def run_block(tick, who, x, weight, kv, mod, gate, cosine, sine, blocks, old):
    vmem = pl.BlockSpec(memory_space=pltpu.VMEM)
    return pl.pallas_call(
        functools.partial(block_kernel, tick),
        out_shape=(
            jax.ShapeDtypeStruct((GROUP, PART), jnp.bfloat16),
            jax.ShapeDtypeStruct((GROUP, 2 * PART), jnp.bfloat16),
        ),
        in_specs=[pl.BlockSpec(memory_space=pltpu.SMEM)] + [vmem] * 9,
        out_specs=(vmem, vmem),
        compiler_params=pltpu.CompilerParams(vmem_limit_bytes=24 * 1024 * 1024),
        name="block_step",
    )(who, x, weight, kv, mod, gate, cosine, sine, blocks, old)


def pick_kernel(place, slots, half_ref, *outs):
    for number in range(3):
        outs[number][...] = half_ref[slots[number * 64 + place[0]]]


def arrange_kernel(place, slots, *refs):
    moved, out = refs[:3], refs[3]
    for j in range(3):
        number = slots[(3 + j) * 64 + place[0]]
        for n in range(3):

            @pl.when(number == n)
            def _():
                out[j] = moved[n][...]


def move_units(kernel, place, units, outs):
    smem = pl.BlockSpec(memory_space=pltpu.SMEM)
    vmem = pl.BlockSpec(memory_space=pltpu.VMEM)
    return pl.pallas_call(
        kernel,
        out_shape=[jax.ShapeDtypeStruct(shape, jnp.bfloat16) for shape in outs],
        in_specs=[smem, smem] + [vmem] * len(units),
        out_specs=[vmem] * len(outs),
        name=kernel.__name__,
    )(place, jnp.asarray(SLOTS), *units)


def body(hidden, timestep, patch_order, modulation, qkv_weight, stale_kv):
    index = {a: lax.axis_index(a) for a in AXES}
    section = index["section"]
    member = index["xl"] * 2 + index["core"]
    place = (((index["xh"] * 2 + index["xl"]) * 4 + index["yh"]) * 2 + index["core"]) * 2 + index["cfg"]
    place = place.astype(jnp.int32).reshape(1)

    columns = jnp.transpose(qkv_weight[0])
    half = lax.dynamic_slice_in_dim(columns, index["cfg"] * SHARE, SHARE, 0).reshape(3, UNIT, D)
    sent = move_units(pick_kernel, place, [half], [(UNIT, D)] * 3)
    moved = [lax.ppermute(sent[number], AXES, ROUTES[number]) for number in range(3)]
    (share,) = move_units(arrange_kernel, place, moved, [(3, UNIT, D)])
    share = lax.all_gather(share.reshape(SHARE, D), "xh", axis=0, tiled=True)
    weight = lax.all_gather(share, ("yh", "cfg"), axis=0, tiled=True)

    share, stale_rows, entering = lax.optimization_barrier((share, stale_kv[0, 0], hidden[0]))
    pieces = [
        jnp.concatenate(
            [stale_rows[:, m * PART : (m + 1) * PART], stale_rows[:, D + m * PART : D + (m + 1) * PART]], axis=1
        )
        for m in range(MEMBERS)
    ]
    pieces = lax.optimization_barrier(jnp.stack(pieces)).reshape(1, 2, 1, 2, LOCAL, 2 * PART)
    outgoing = jnp.broadcast_to(pieces, (2, 2, 4, 2, LOCAL, 2 * PART)).reshape(32, LOCAL, 2 * PART)
    kv = lax.all_to_all(outgoing, ("xh", "xl", "yh", "core"), split_axis=0, concat_axis=0, tiled=True)
    kv = kv.reshape(TOKENS, 2 * PART)

    x = lax.all_gather(entering, ("xl", "core"), axis=0, tiled=True)
    x = jnp.transpose(x.reshape(GROUP, MEMBERS, PART), (1, 0, 2))

    row = lax.dynamic_index_in_dim(modulation[0, 0], timestep[0], 0, keepdims=False)
    mod = row[: 2 * D].reshape(2, D)
    gate = lax.dynamic_slice_in_dim(row, 2 * D + member * PART, PART, 0).reshape(1, PART)

    lane = jnp.arange(GROUP, dtype=jnp.int32)
    source = lane // LOCAL
    patch = ((index["xh"] * 2 + source // 2) * 4 + index["yh"]) * 2 + source % 2
    blocks = patch * (LOCAL // ROWS) + lane % LOCAL // ROWS
    positions = (patch_order[blocks] * ROWS + lane % ROWS).astype(jnp.float32)
    halfway = HDIM // 2
    inverse = jnp.exp(-math.log(10000.0) * jnp.arange(halfway, dtype=jnp.float32) / halfway)
    angles = positions[:, None] * inverse[None, :]
    cosine, sine = jnp.cos(angles), jnp.sin(angles)
    cosine = jnp.concatenate([cosine, cosine], axis=1)
    sine = jnp.concatenate([-sine, sine], axis=1)

    who = jnp.stack([member, section]).astype(jnp.int32)
    fresh = jnp.zeros((GROUP, 2 * PART), jnp.bfloat16)
    for tick in range(SECTIONS):
        state, fresh = run_block(tick, who, x, weight, kv, mod, gate, cosine, sine, blocks[:, None], fresh)
        if tick + 1 < SECTIONS:
            state = lax.all_gather(state, "section", axis=0, tiled=False, axis_index_groups=PAIRS[tick % 2])[0]
            x = lax.all_gather(state, ("xl", "core"), axis=0, tiled=False)

    ends = lax.all_gather(state, ("xl", "core"), axis=0, tiled=False)
    ends, fresh = lax.optimization_barrier((ends, fresh))
    finals = lax.dynamic_slice_in_dim(ends, member * LOCAL, LOCAL, 1)
    finals = jnp.transpose(finals, (1, 0, 2)).reshape(SECTIONS, LOCAL // SECTIONS, 2, D // 2)
    finals = jnp.transpose(finals, (0, 2, 1, 3)).reshape(SECTIONS * 2, LOCAL // SECTIONS, D // 2)
    spread = lax.all_to_all(finals, ("section", "cfg"), split_axis=0, concat_axis=0, tiled=True)
    kept = lax.all_gather(fresh, ("xl", "core"), axis=0, tiled=False)
    kept = lax.dynamic_slice_in_dim(kept, member * LOCAL, LOCAL, 1)
    kept = jnp.transpose(kept.reshape(MEMBERS, LOCAL, 2, PART), (1, 2, 0, 3)).reshape(LOCAL, 2 * D)
    uncond = spread[2 * SECTIONS - 2].astype(jnp.float32)
    conditioned = spread[2 * SECTIONS - 1].astype(jnp.float32)
    guided = (uncond + guide_weight * (conditioned - uncond)).astype(jnp.bfloat16)
    return guided, kept[None, None]


def solution(mesh):
    fine = Mesh(mesh.devices.reshape(SIZES), AXES)
    patch = ("xh", "xl", "yh", "core")
    return jax.shard_map(
        body,
        mesh=fine,
        in_specs=(
            P("cfg", patch, None),
            P(),
            P(),
            P("section", "cfg", None, None),
            P("section", None, patch),
            P("section", "cfg", patch, None),
        ),
        out_specs=(P((*patch, "section"), "cfg"), P("section", "cfg", patch, None)),
        check_vma=False,
    )
```

```python
import functools
import math

import jax
import jax.numpy as jnp
import numpy as np
from jax import lax
from jax.experimental import pallas as pl
from jax.experimental.pallas import tpu as pltpu
from jax.sharding import Mesh, PartitionSpec as P

HEADS = 12
HDIM = 128
ROWS = 8
D = HEADS * HDIM
TOKENS = 512
SECTIONS = 8
MEMBERS = 4
PART = D // MEMBERS
LOCAL = 16
GROUP = LOCAL * MEMBERS
UNIT = 48
UNITS = 3
COLUMNS = UNIT * UNITS
HALF = D // 2
BLOCK = 2 * COLUMNS

guide_weight = 3.5
norm_eps = 1e-06

AXES = ("xh", "xl", "yh", "core", "section", "cfg")
SIZES = (2, 2, 4, 2, 8, 2)


def route(step):
    def number(x, y, core, section):
        return (((x * 4 + y // 2) * 2 + core) * 8 + section) * 2 + y % 2

    return [
        (number(x, y, core, s), number(*step(x, y, core), s))
        for x in range(4)
        for y in range(8)
        for core in range(2)
        for s in range(SECTIONS)
    ]


SWAP = route(lambda x, y, core: (x, y, 1 - core))
UP = route(lambda x, y, core: (x, (y + 1) % 8, core))
DOWN = route(lambda x, y, core: (x, (y - 1) % 8, core))
STARTS = np.zeros((MEMBERS, 3), np.int32)
for _member in range(MEMBERS):
    for _third in range(3):
        STARTS[_member, (COLUMNS * 8 * ((_third - _member) % 4) + PART * _third) // D] = PART * _third
PAIRS = (
    [[s, s + 1] for s in range(0, SECTIONS, 2)],
    [[s, (s + 1) % SECTIONS] for s in range(1, SECTIONS, 2)],
)


def nt_dot(a, b):
    return lax.dot_general(a, b, (((1,), (1,)), ((), ())), preferred_element_type=jnp.float32)


def block_kernel(tick, who, x_ref, w_ref, kv_ref, mod_ref, gate_ref, cos_ref, sin_ref, block_ref, old_ref, state_ref, fresh_ref, projected):
    member = who[0]
    active = who[1] == tick
    xs = [x_ref[i].astype(jnp.float32) for i in range(MEMBERS)]
    center = sum(jnp.sum(x, axis=-1, keepdims=True) for x in xs) / D
    xs = [x - center for x in xs]
    spread = sum(jnp.sum(x * x, axis=-1, keepdims=True) for x in xs) / D
    inv = lax.rsqrt(spread + norm_eps)
    normed = jnp.concatenate(
        [
            (
                xs[i] * inv * (1.0 + mod_ref[1:2, i * PART : (i + 1) * PART])
                + mod_ref[0:1, i * PART : (i + 1) * PART]
            ).astype(jnp.bfloat16)
            for i in range(MEMBERS)
        ],
        axis=1,
    )
    projected[...] = nt_dot(normed, w_ref[...]).astype(jnp.bfloat16)
    row_block = block_ref[...]
    stale_mask = lax.broadcasted_iota(jnp.int32, (GROUP, TOKENS), 1) // ROWS == row_block
    own_mask = (
        lax.broadcasted_iota(jnp.int32, (GROUP, GROUP), 0) // ROWS
        == lax.broadcasted_iota(jnp.int32, (GROUP, GROUP), 1) // ROWS
    )
    cosine, sine = cos_ref[...], sin_ref[...]

    def turned(values):
        values = values.astype(jnp.float32)
        values = values * lax.rsqrt(jnp.mean(values * values, axis=-1, keepdims=True) + norm_eps)
        return (values * cosine + pltpu.roll(values, HDIM // 2, 1) * sine).astype(jnp.bfloat16)

    scale = 1.0 / math.sqrt(HDIM)
    for head in range(PART // HDIM):
        cols = slice(head * HDIM, (head + 1) * HDIM)
        query, key, value = (
            projected[:, pl.ds(pl.multiple_of(who[2 + part] + head * HDIM, HDIM), HDIM)] for part in range(3)
        )
        query, key = turned(query), turned(key)
        weights = jnp.where(stale_mask, 0.0, jnp.exp(nt_dot(query, kv_ref[:, cols]) * scale))
        own = jnp.where(own_mask, jnp.exp(nt_dot(query, key) * scale), 0.0)
        total = jnp.sum(weights, axis=-1, keepdims=True) + jnp.sum(own, axis=-1, keepdims=True)
        attended = jnp.dot(
            weights.astype(jnp.bfloat16),
            kv_ref[:, PART + head * HDIM : PART + (head + 1) * HDIM],
            preferred_element_type=jnp.float32,
        ) + jnp.dot(own.astype(jnp.bfloat16), value, preferred_element_type=jnp.float32)
        attended = attended / total
        state = x_ref[member, :, cols].astype(jnp.float32) + gate_ref[0:1, cols] * attended
        state_ref[:, cols] = state.astype(jnp.bfloat16)
        fresh_ref[:, cols] = jnp.where(active, key, old_ref[:, cols])
        vcols = slice(PART + head * HDIM, PART + (head + 1) * HDIM)
        fresh_ref[:, vcols] = jnp.where(active, value, old_ref[:, vcols])


def run_block(tick, who, x, weight, kv, mod, gate, cosine, sine, blocks, old):
    vmem = pl.BlockSpec(memory_space=pltpu.VMEM)
    return pl.pallas_call(
        functools.partial(block_kernel, tick),
        out_shape=(
            jax.ShapeDtypeStruct((GROUP, PART), jnp.bfloat16),
            jax.ShapeDtypeStruct((GROUP, 2 * PART), jnp.bfloat16),
        ),
        in_specs=[pl.BlockSpec(memory_space=pltpu.SMEM)] + [vmem] * 9,
        out_specs=(vmem, vmem),
        scratch_shapes=[pltpu.VMEM((GROUP, 3 * PART), jnp.bfloat16)],
        compiler_params=pltpu.CompilerParams(vmem_limit_bytes=24 * 1024 * 1024),
        name="block_step",
    )(who, x, weight, kv, mod, gate, cosine, sine, blocks, old)


def pick_kernel(where, x_ref, keep_ref, send_ref):
    member, first, core = where[0], where[1], where[2]
    peer = member + 1 - 2 * core
    for j in range(UNITS):
        third = (first + j * UNIT) // PART
        keep_ref[j * UNIT : (j + 1) * UNIT, :] = x_ref[(third - member + 4) % 4, j * UNIT : (j + 1) * UNIT, :]
        send_ref[j * UNIT : (j + 1) * UNIT, :] = x_ref[(third - peer + 4) % 4, j * UNIT : (j + 1) * UNIT, :]


def place_kernel(where, own, up1, up2, up3, down1, down2, down3, up4, down4, out_ref):
    core, y = where[2], where[3]

    def put(source, part, ref):
        at = (y + source + 8) % 8
        row = pl.multiple_of(at // 2 * BLOCK + (core + part) % 2 * COLUMNS, 16)
        col = pl.multiple_of(at % 2 * HALF, 128)
        out_ref[pl.ds(row, COLUMNS), pl.ds(col, HALF)] = ref[...]

    for source, ref in ((0, own), (-1, up1), (-2, up2), (-3, up3), (1, down1), (2, down2), (3, down3)):
        put(source, 0, ref.at[:COLUMNS])
        put(source, 1, ref.at[COLUMNS:])
    put(4, 0, up4)
    put(4, 1, down4)


def whole_call(kernel, where, arrays, outs):
    vmem = pl.BlockSpec(memory_space=pltpu.VMEM)
    return pl.pallas_call(
        kernel,
        out_shape=[jax.ShapeDtypeStruct(shape, jnp.bfloat16) for shape in outs],
        in_specs=[pl.BlockSpec(memory_space=pltpu.SMEM)] + [vmem] * len(arrays),
        out_specs=[vmem] * len(outs),
        compiler_params=pltpu.CompilerParams(vmem_limit_bytes=24 * 1024 * 1024),
        name=kernel.__name__,
    )(where, *arrays)


def body(hidden, timestep, patch_order, modulation, qkv_weight, stale_kv):
    index = {a: lax.axis_index(a) for a in AXES}
    section = index["section"]
    member = index["xl"] * 2 + index["core"]
    y = index["yh"] * 2 + index["cfg"]
    first = (index["yh"] * 2 + index["core"]) * COLUMNS
    starts = jnp.asarray(STARTS)[member]
    where = jnp.stack([member, first, index["core"], y]).astype(jnp.int32)
    who = jnp.concatenate([jnp.stack([member, section]).astype(jnp.int32), starts])

    columns = lax.dynamic_slice_in_dim(jnp.transpose(qkv_weight[0]), index["cfg"] * HALF, HALF, 1)
    columns = lax.all_gather(columns, ("xh", "xl"), axis=0, tiled=False)
    keep, send = whole_call(pick_kernel, where, [columns], [(COLUMNS, HALF)] * 2)
    own = jnp.concatenate([keep, lax.ppermute(send, AXES, SWAP)])
    own, stale_rows = lax.optimization_barrier((own, stale_kv[0, 0]))
    up, down = [own], [own]
    for _ in range(3):
        up.append(lax.ppermute(up[-1], AXES, UP))
        down.append(lax.ppermute(down[-1], AXES, DOWN))
    up4 = lax.ppermute(up[3][:COLUMNS], AXES, UP)
    down4 = lax.ppermute(down[3][COLUMNS:], AXES, DOWN)
    (weight,) = whole_call(place_kernel, where, [own, *up[1:], *down[1:], up4, down4], [(3 * PART, D)])

    pieces = [
        jnp.concatenate(
            [stale_rows[:, m * PART : (m + 1) * PART], stale_rows[:, D + m * PART : D + (m + 1) * PART]], axis=1
        )
        for m in range(MEMBERS)
    ]
    pieces = lax.optimization_barrier(jnp.stack(pieces)).reshape(1, 2, 1, 2, LOCAL, 2 * PART)
    outgoing = jnp.broadcast_to(pieces, (2, 2, 4, 2, LOCAL, 2 * PART)).reshape(32, LOCAL, 2 * PART)
    kv = lax.all_to_all(outgoing, ("xh", "xl", "yh", "core"), split_axis=0, concat_axis=0, tiled=True)
    kv = kv.reshape(TOKENS, 2 * PART)

    entering, _ = lax.optimization_barrier((hidden[0], up[1]))
    x = lax.all_gather(entering, ("xl", "core"), axis=0, tiled=True)
    x = jnp.transpose(x.reshape(GROUP, MEMBERS, PART), (1, 0, 2))

    row = lax.dynamic_index_in_dim(modulation[0, 0], timestep[0], 0, keepdims=False)
    mod = row[: 2 * D].reshape(2, D)
    gate = lax.dynamic_slice_in_dim(row, 2 * D + member * PART, PART, 0).reshape(1, PART)

    lane = jnp.arange(GROUP, dtype=jnp.int32)
    source = lane // LOCAL
    patch = ((index["xh"] * 2 + source // 2) * 4 + index["yh"]) * 2 + source % 2
    blocks = patch * (LOCAL // ROWS) + lane % LOCAL // ROWS
    positions = (patch_order[blocks] * ROWS + lane % ROWS).astype(jnp.float32)
    halfway = HDIM // 2
    inverse = jnp.exp(-math.log(10000.0) * jnp.arange(halfway, dtype=jnp.float32) / halfway)
    angles = positions[:, None] * inverse[None, :]
    cosine, sine = jnp.cos(angles), jnp.sin(angles)
    cosine = jnp.concatenate([cosine, cosine], axis=1)
    sine = jnp.concatenate([-sine, sine], axis=1)

    fresh = jnp.zeros((GROUP, 2 * PART), jnp.bfloat16)
    for tick in range(SECTIONS):
        state, fresh = run_block(tick, who, x, weight, kv, mod, gate, cosine, sine, blocks[:, None], fresh)
        if tick + 1 < SECTIONS:
            state = lax.all_gather(state, "section", axis=0, tiled=False, axis_index_groups=PAIRS[tick % 2])[0]
            x = lax.all_gather(state, ("xl", "core"), axis=0, tiled=False)

    ends = lax.all_gather(state, ("xl", "core"), axis=0, tiled=False)
    ends, fresh = lax.optimization_barrier((ends, fresh))
    finals = lax.dynamic_slice_in_dim(ends, member * LOCAL, LOCAL, 1)
    finals = jnp.transpose(finals, (1, 0, 2)).reshape(SECTIONS, LOCAL // SECTIONS, 2, D // 2)
    finals = jnp.transpose(finals, (0, 2, 1, 3)).reshape(SECTIONS * 2, LOCAL // SECTIONS, D // 2)
    spread = lax.all_to_all(finals, ("section", "cfg"), split_axis=0, concat_axis=0, tiled=True)
    kept = lax.all_gather(fresh, ("xl", "core"), axis=0, tiled=False)
    kept = lax.dynamic_slice_in_dim(kept, member * LOCAL, LOCAL, 1)
    kept = jnp.transpose(kept.reshape(MEMBERS, LOCAL, 2, PART), (1, 2, 0, 3)).reshape(LOCAL, 2 * D)
    uncond = spread[2 * SECTIONS - 2].astype(jnp.float32)
    conditioned = spread[2 * SECTIONS - 1].astype(jnp.float32)
    guided = (uncond + guide_weight * (conditioned - uncond)).astype(jnp.bfloat16)
    return guided, kept[None, None]


def solution(mesh):
    fine = Mesh(mesh.devices.reshape(SIZES), AXES)
    patch = ("xh", "xl", "yh", "core")
    return jax.shard_map(
        body,
        mesh=fine,
        in_specs=(
            P("cfg", patch, None),
            P(),
            P(),
            P("section", "cfg", None, None),
            P("section", None, patch),
            P("section", "cfg", patch, None),
        ),
        out_specs=(P((*patch, "section"), "cfg"), P("section", "cfg", patch, None)),
        check_vma=False,
    )
```

```python
import functools
import math

import jax
import jax.numpy as jnp
import numpy as np
from jax import lax
from jax.experimental import pallas as pl
from jax.experimental.pallas import tpu as pltpu
from jax.sharding import Mesh, PartitionSpec as P

HEADS = 12
HDIM = 128
ROWS = 8
D = HEADS * HDIM
TOKENS = 512
SECTIONS = 8
MEMBERS = 4
PART = D // MEMBERS
LOCAL = 16
GROUP = LOCAL * MEMBERS
UNIT = 48
UNITS = 3
COLUMNS = UNIT * UNITS
HALF = D // 2
BLOCK = 2 * COLUMNS

guide_weight = 3.5
norm_eps = 1e-06

AXES = ("xh", "xl", "yh", "core", "section", "cfg")
SIZES = (2, 2, 4, 2, 8, 2)


def route(step):
    def number(x, y, core, section):
        return (((x * 4 + y // 2) * 2 + core) * 8 + section) * 2 + y % 2

    return [
        (number(x, y, core, s), number(*step(x, y, core), s))
        for x in range(4)
        for y in range(8)
        for core in range(2)
        for s in range(SECTIONS)
    ]


SWAP = route(lambda x, y, core: (x, y, 1 - core))
UP = route(lambda x, y, core: (x, (y + 1 - 2 * core) % 8, core))
DOWN = route(lambda x, y, core: (x, (y - 1 + 2 * core) % 8, core))
ACROSS = [(i, (i + 256) % 512) for i in range(512)]
PAIRS = (
    [[s, s + 1] for s in range(0, SECTIONS, 2)],
    [[s, (s + 1) % SECTIONS] for s in range(1, SECTIONS, 2)],
)


def nt_dot(a, b):
    return lax.dot_general(a, b, (((1,), (1,)), ((), ())), preferred_element_type=jnp.float32)


def block_kernel(tick, who, x_ref, w_ref, kv_ref, other_ref, mod_ref, gate_ref, cos_ref, sin_ref, block_ref, old_ref, state_ref, fresh_ref):
    member = who[0]
    active = who[1] == tick
    xs = [x_ref[i].astype(jnp.float32) for i in range(MEMBERS)]
    center = sum(jnp.sum(x, axis=-1, keepdims=True) for x in xs) / D
    xs = [x - center for x in xs]
    spread = sum(jnp.sum(x * x, axis=-1, keepdims=True) for x in xs) / D
    inv = lax.rsqrt(spread + norm_eps)
    normed = jnp.concatenate(
        [
            (
                xs[i] * inv * (1.0 + mod_ref[1:2, i * PART : (i + 1) * PART])
                + mod_ref[0:1, i * PART : (i + 1) * PART]
            ).astype(jnp.bfloat16)
            for i in range(MEMBERS)
        ],
        axis=1,
    )
    projected = jnp.dot(normed, w_ref[...], preferred_element_type=jnp.float32).astype(jnp.bfloat16)
    row_block = block_ref[...]
    stale_mask = lax.broadcasted_iota(jnp.int32, (GROUP, TOKENS // 2), 1) // ROWS == row_block
    own_mask = (
        lax.broadcasted_iota(jnp.int32, (GROUP, GROUP), 0) // ROWS
        == lax.broadcasted_iota(jnp.int32, (GROUP, GROUP), 1) // ROWS
    )
    cosine, sine = cos_ref[...], sin_ref[...]

    def turned(values):
        values = values.astype(jnp.float32)
        values = values * lax.rsqrt(jnp.mean(values * values, axis=-1, keepdims=True) + norm_eps)
        return (values * cosine + pltpu.roll(values, HDIM // 2, 1) * sine).astype(jnp.bfloat16)

    heads = range(PART // HDIM)
    cols = [slice(h * HDIM, (h + 1) * HDIM) for h in heads]
    vcols = [slice(PART + h * HDIM, PART + (h + 1) * HDIM) for h in heads]
    scale = 1.0 / math.sqrt(HDIM)
    query = [turned(projected[:, cols[h]]) for h in heads]
    key = [turned(projected[:, vcols[h]]) for h in heads]
    value = [projected[:, 2 * PART + h * HDIM : 2 * PART + (h + 1) * HDIM] for h in heads]
    scores = [nt_dot(query[h], kv_ref[:, cols[h]]) for h in heads]
    other_scores = [nt_dot(query[h], other_ref[:, cols[h]]) for h in heads]
    own_scores = [nt_dot(query[h], key[h]) for h in heads]
    weights = [jnp.where(stale_mask, 0.0, jnp.exp(scores[h] * scale)) for h in heads]
    others = [jnp.exp(other_scores[h] * scale) for h in heads]
    own = [jnp.where(own_mask, jnp.exp(own_scores[h] * scale), 0.0) for h in heads]
    total = [
        jnp.sum(weights[h] + others[h], axis=-1, keepdims=True) + jnp.sum(own[h], axis=-1, keepdims=True)
        for h in heads
    ]
    attended = [
        jnp.dot(weights[h].astype(jnp.bfloat16), kv_ref[:, vcols[h]], preferred_element_type=jnp.float32)
        + jnp.dot(others[h].astype(jnp.bfloat16), other_ref[:, vcols[h]], preferred_element_type=jnp.float32)
        + jnp.dot(own[h].astype(jnp.bfloat16), value[h], preferred_element_type=jnp.float32)
        for h in heads
    ]
    for h in heads:
        state = x_ref[member, :, cols[h]].astype(jnp.float32) + gate_ref[0:1, cols[h]] * (attended[h] / total[h])
        state_ref[:, cols[h]] = state.astype(jnp.bfloat16)
        fresh_ref[:, cols[h]] = jnp.where(active, key[h], old_ref[:, cols[h]])
        fresh_ref[:, vcols[h]] = jnp.where(active, value[h], old_ref[:, vcols[h]])


def run_block(tick, who, x, weight, kv, other, mod, gate, cosine, sine, blocks, old):
    vmem = pl.BlockSpec(memory_space=pltpu.VMEM)
    weight = pltpu.with_memory_space_constraint(weight, pltpu.VMEM)
    return pl.pallas_call(
        functools.partial(block_kernel, tick),
        out_shape=(
            jax.ShapeDtypeStruct((GROUP, PART), jnp.bfloat16),
            jax.ShapeDtypeStruct((GROUP, 2 * PART), jnp.bfloat16),
        ),
        in_specs=[pl.BlockSpec(memory_space=pltpu.SMEM)] + [vmem] * 10,
        out_specs=(vmem, vmem),
        compiler_params=pltpu.CompilerParams(vmem_limit_bytes=24 * 1024 * 1024),
        name="block_step",
    )(who, x, weight, kv, other, mod, gate, cosine, sine, blocks, old)


def prepare_kernel(where, stale_ref, columns_ref, out_ref, half_ref):
    for slot in range(2 * 4 * 2):
        m = slot // 8 * 2 + slot % 2
        out_ref[slot, :, :PART] = stale_ref[:, m * PART : (m + 1) * PART]
        out_ref[slot, :, PART:] = stale_ref[:, D + m * PART : D + (m + 1) * PART]
    half_ref[...] = columns_ref[:, pl.ds(pl.multiple_of(where[3] % 2 * HALF, 128), HALF)]


def pick_kernel(where, x_ref, keep_ref, send_ref):
    member, first, core = where[0], where[1], where[2]
    peer = member + 1 - 2 * core
    for j in range(UNITS):
        third = (first + j * UNIT) // PART
        keep_ref[j * UNIT : (j + 1) * UNIT, :] = x_ref[(third - member + 4) % 4, j * UNIT : (j + 1) * UNIT, :]
        send_ref[j * UNIT : (j + 1) * UNIT, :] = x_ref[(third - peer + 4) % 4, j * UNIT : (j + 1) * UNIT, :]


def place_kernel(where, own, up1, up2, up3, down1, down2, down3, up4, down4, out_ref, rows, sem):
    member, core, y = where[0], where[2], where[3]
    sign = 1 - 2 * core
    copies = []

    def home(unit):
        third = unit // 8
        part = (COLUMNS * 8 * ((third - member + 4) % 4) + PART * third) // D
        return part * PART + unit % 8 * UNIT

    def put(source, part, ref, begin):
        at = (y + sign * source + 8) % 8
        first = (at // 2 * 2 + (core + part) % 2) * UNITS
        for j in range(UNITS):
            unit = first + j
            row = pl.multiple_of(home(unit), 16)
            col = pl.multiple_of(at % 2 * HALF, 128)
            copy = pltpu.make_async_copy(
                ref.at[pl.ds(begin + j * UNIT, UNIT)], rows.at[pl.ds(row, UNIT), pl.ds(col, HALF)], sem
            )
            copy.start()
            copies.append(copy)

    for source, ref in ((0, own), (-1, up1), (-2, up2), (-3, up3), (1, down1), (2, down2), (3, down3)):
        put(source, 0, ref, 0)
        put(source, 1, ref, COLUMNS)
    put(4, 0, up4, 0)
    put(4, 1, down4, 0)
    for copy in copies:
        copy.wait()
    for c in range(0, D, HDIM):
        out_ref[c : c + HDIM, :] = jnp.transpose(rows[:, c : c + HDIM])


def place(where, blocks):
    return pl.pallas_call(
        place_kernel,
        out_shape=jax.ShapeDtypeStruct((D, 3 * PART), jnp.bfloat16),
        in_specs=[pl.BlockSpec(memory_space=pltpu.SMEM)] + [pl.BlockSpec(memory_space=pl.ANY)] * len(blocks),
        out_specs=pl.BlockSpec(memory_space=pltpu.VMEM),
        scratch_shapes=[pltpu.VMEM((3 * PART, D), jnp.bfloat16), pltpu.SemaphoreType.DMA],
        compiler_params=pltpu.CompilerParams(vmem_limit_bytes=12 * 1024 * 1024),
        name="place_weight",
    )(where, *blocks)


def whole_call(kernel, where, arrays, outs):
    vmem = pl.BlockSpec(memory_space=pltpu.VMEM)
    return pl.pallas_call(
        kernel,
        out_shape=[jax.ShapeDtypeStruct(shape, jnp.bfloat16) for shape in outs],
        in_specs=[pl.BlockSpec(memory_space=pltpu.SMEM)] + [vmem] * len(arrays),
        out_specs=[vmem] * len(outs),
        compiler_params=pltpu.CompilerParams(vmem_limit_bytes=24 * 1024 * 1024),
        name=kernel.__name__,
    )(where, *arrays)


def body(hidden, timestep, patch_order, modulation, qkv_weight, stale_kv):
    index = {a: lax.axis_index(a) for a in AXES}
    section = index["section"]
    member = index["xl"] * 2 + index["core"]
    y = index["yh"] * 2 + index["cfg"]
    first = (index["yh"] * 2 + index["core"]) * COLUMNS
    where = jnp.stack([member, first, index["core"], y]).astype(jnp.int32)
    who = jnp.stack([member, section]).astype(jnp.int32)

    outgoing, columns = whole_call(
        prepare_kernel,
        where,
        [stale_kv[0, 0], jnp.transpose(qkv_weight[0])],
        [(2 * 4 * 2, LOCAL, 2 * PART), (COLUMNS, HALF)],
    )
    kv = lax.all_to_all(outgoing, ("xl", "yh", "core"), split_axis=0, concat_axis=0, tiled=True)
    kv = kv.reshape(TOKENS // 2, 2 * PART)

    columns = lax.all_gather(columns, ("xh", "xl"), axis=0, tiled=False)
    keep, send = whole_call(pick_kernel, where, [columns], [(COLUMNS, HALF)] * 2)
    own = jnp.concatenate([keep, lax.ppermute(send, AXES, SWAP)])
    own, kv = lax.optimization_barrier((own, kv))
    up1, down1 = lax.ppermute(own, AXES, UP), lax.ppermute(own, AXES, DOWN)
    up1, entering, kv = lax.optimization_barrier((up1, hidden[0], kv))
    kv_other = lax.ppermute(kv, AXES, ACROSS)
    x = lax.all_gather(entering, ("xl", "core"), axis=0, tiled=True)
    up2, down2 = lax.ppermute(up1, AXES, UP), lax.ppermute(down1, AXES, DOWN)
    down2, x = lax.optimization_barrier((down2, x))
    up3, down3 = lax.ppermute(up2, AXES, UP), lax.ppermute(down2, AXES, DOWN)
    up4 = lax.ppermute(up3[:COLUMNS], AXES, UP)
    down4 = lax.ppermute(down3[COLUMNS:], AXES, DOWN)
    weight = place(where, [own, up1, up2, up3, down1, down2, down3, up4, down4])
    x = jnp.transpose(x.reshape(GROUP, MEMBERS, PART), (1, 0, 2))

    row = lax.dynamic_index_in_dim(modulation[0, 0], timestep[0], 0, keepdims=False)
    mod = row[: 2 * D].reshape(2, D)
    gate = lax.dynamic_slice_in_dim(row, 2 * D + member * PART, PART, 0).reshape(1, PART)

    lane = jnp.arange(GROUP, dtype=jnp.int32)
    source = lane // LOCAL
    patch = (source // 2 * 4 + index["yh"]) * 2 + source % 2
    blocks = patch * (LOCAL // ROWS) + lane % LOCAL // ROWS
    positions = (patch_order[index["xh"] * (TOKENS // 2 // ROWS) + blocks] * ROWS + lane % ROWS).astype(jnp.float32)
    halfway = HDIM // 2
    inverse = jnp.exp(-math.log(10000.0) * jnp.arange(halfway, dtype=jnp.float32) / halfway)
    angles = positions[:, None] * inverse[None, :]
    cosine, sine = jnp.cos(angles), jnp.sin(angles)
    cosine = jnp.concatenate([cosine, cosine], axis=1)
    sine = jnp.concatenate([-sine, sine], axis=1)

    fresh = jnp.zeros((GROUP, 2 * PART), jnp.bfloat16)
    for tick in range(SECTIONS):
        state, fresh = run_block(tick, who, x, weight, kv, kv_other, mod, gate, cosine, sine, blocks[:, None], fresh)
        if tick + 1 < SECTIONS:
            state = lax.all_gather(state, "section", axis=0, tiled=False, axis_index_groups=PAIRS[tick % 2])[0]
            x = lax.all_gather(state, ("xl", "core"), axis=0, tiled=False)

    ends = lax.all_gather(state, ("xl", "core"), axis=0, tiled=False)
    finals = lax.dynamic_slice_in_dim(ends, member * LOCAL, LOCAL, 1)
    finals = jnp.transpose(finals, (1, 0, 2)).reshape(SECTIONS, LOCAL // SECTIONS, 2, D // 2)
    finals = jnp.transpose(finals, (0, 2, 1, 3)).reshape(SECTIONS * 2, LOCAL // SECTIONS, D // 2)
    spread = lax.all_to_all(finals, ("section", "cfg"), split_axis=0, concat_axis=0, tiled=True)
    kept = lax.all_gather(fresh, ("xl", "core"), axis=0, tiled=False)
    spread, kept = lax.optimization_barrier((spread, kept))
    kept = lax.dynamic_slice_in_dim(kept, member * LOCAL, LOCAL, 1)
    kept = jnp.transpose(kept.reshape(MEMBERS, LOCAL, 2, PART), (1, 2, 0, 3)).reshape(LOCAL, 2 * D)
    uncond = spread[2 * SECTIONS - 2].astype(jnp.float32)
    conditioned = spread[2 * SECTIONS - 1].astype(jnp.float32)
    guided = (uncond + guide_weight * (conditioned - uncond)).astype(jnp.bfloat16)
    return guided, kept[None, None]


def solution(mesh):
    fine = Mesh(mesh.devices.reshape(SIZES), AXES)
    patch = ("xh", "xl", "yh", "core")
    return jax.shard_map(
        body,
        mesh=fine,
        in_specs=(
            P("cfg", patch, None),
            P(),
            P(),
            P("section", "cfg", None, None),
            P("section", None, patch),
            P("section", "cfg", patch, None),
        ),
        out_specs=(P((*patch, "section"), "cfg"), P("section", "cfg", patch, None)),
        check_vma=False,
    )
```

```python
import functools
import math

import jax
import jax.numpy as jnp
import numpy as np
from jax import lax
from jax.experimental import pallas as pl
from jax.experimental.pallas import tpu as pltpu
from jax.sharding import Mesh, PartitionSpec as P

HEADS = 12
HDIM = 128
ROWS = 8
D = HEADS * HDIM
TOKENS = 512
SECTIONS = 8
MEMBERS = 4
PART = D // MEMBERS
LOCAL = 16
GROUP = LOCAL * MEMBERS
UNIT = 48
UNITS = 3
COLUMNS = UNIT * UNITS
HALF = D // 2
BLOCK = 2 * COLUMNS

guide_weight = 3.5
norm_eps = 1e-06

AXES = ("xh", "xl", "yh", "core", "section", "cfg")
SIZES = (2, 2, 4, 2, 8, 2)


def route(step):
    def number(x, y, core, section):
        return (((x * 4 + y // 2) * 2 + core) * 8 + section) * 2 + y % 2

    return [
        (number(x, y, core, s), number(*step(x, y, core), s))
        for x in range(4)
        for y in range(8)
        for core in range(2)
        for s in range(SECTIONS)
    ]


SWAP = route(lambda x, y, core: (x, y, 1 - core))
UP = route(lambda x, y, core: (x, (y + 1 - 2 * core) % 8, core))
DOWN = route(lambda x, y, core: (x, (y - 1 + 2 * core) % 8, core))
ACROSS = [(i, (i + 256) % 512) for i in range(512)]


def onward(section, flip):
    def number(x, y, core, s):
        return (((x * 4 + y // 2) * 2 + core) * 8 + s) * 2 + y % 2

    return [
        (number(x, y, core, section), number(x ^ flip, y, core, section + 1))
        for x in range(4)
        for y in range(8)
        for core in range(2)
    ]


def nt_dot(a, b):
    return lax.dot_general(a, b, (((1,), (1,)), ((), ())), preferred_element_type=jnp.float32)


def block_kernel(tick, who, near_ref, far_ref, w_ref, kv_ref, other_ref, mod_ref, gate_ref, cos_ref, sin_ref, block_ref, old_ref, state_ref, fresh_ref):
    active = who[1] == tick

    @pl.when(jnp.logical_not(active))
    def _():
        fresh_ref[...] = old_ref[...]

    @pl.when(active)
    def _():
        active_block(who[0], near_ref, far_ref, w_ref, kv_ref, other_ref, mod_ref, gate_ref, cos_ref, sin_ref, block_ref, state_ref, fresh_ref)


def active_block(member, near_ref, far_ref, w_ref, kv_ref, other_ref, mod_ref, gate_ref, cos_ref, sin_ref, block_ref, state_ref, fresh_ref):
    near = [near_ref[core].astype(jnp.float32) for core in range(2)]
    far = [far_ref[core].astype(jnp.float32) for core in range(2)]
    low = member < 2
    xs = [jnp.where(low, near[core], far[core]) for core in range(2)]
    xs += [jnp.where(low, far[core], near[core]) for core in range(2)]
    center = sum(jnp.sum(x, axis=-1, keepdims=True) for x in xs) / D
    xs = [x - center for x in xs]
    spread = sum(jnp.sum(x * x, axis=-1, keepdims=True) for x in xs) / D
    inv = lax.rsqrt(spread + norm_eps)
    normed = jnp.concatenate(
        [
            (
                xs[i] * inv * (1.0 + mod_ref[1:2, i * PART : (i + 1) * PART])
                + mod_ref[0:1, i * PART : (i + 1) * PART]
            ).astype(jnp.bfloat16)
            for i in range(MEMBERS)
        ],
        axis=1,
    )
    projected = jnp.dot(normed, w_ref[...], preferred_element_type=jnp.float32).astype(jnp.bfloat16)
    row_block = block_ref[...]
    stale_mask = lax.broadcasted_iota(jnp.int32, (GROUP, TOKENS // 2), 1) // ROWS == row_block
    own_mask = (
        lax.broadcasted_iota(jnp.int32, (GROUP, GROUP), 0) // ROWS
        == lax.broadcasted_iota(jnp.int32, (GROUP, GROUP), 1) // ROWS
    )
    cosine, sine = cos_ref[...], sin_ref[...]

    def turned(values):
        values = values.astype(jnp.float32)
        values = values * lax.rsqrt(jnp.mean(values * values, axis=-1, keepdims=True) + norm_eps)
        return (values * cosine + pltpu.roll(values, HDIM // 2, 1) * sine).astype(jnp.bfloat16)

    heads = range(PART // HDIM)
    cols = [slice(h * HDIM, (h + 1) * HDIM) for h in heads]
    vcols = [slice(PART + h * HDIM, PART + (h + 1) * HDIM) for h in heads]
    scale = 1.0 / math.sqrt(HDIM)
    query = [turned(projected[:, cols[h]]) for h in heads]
    key = [turned(projected[:, vcols[h]]) for h in heads]
    value = [projected[:, 2 * PART + h * HDIM : 2 * PART + (h + 1) * HDIM] for h in heads]
    scores = [nt_dot(query[h], kv_ref[:, cols[h]]) for h in heads]
    other_scores = [nt_dot(query[h], other_ref[:, cols[h]]) for h in heads]
    own_scores = [nt_dot(query[h], key[h]) for h in heads]
    weights = [jnp.where(stale_mask, 0.0, jnp.exp(scores[h] * scale)) for h in heads]
    others = [jnp.exp(other_scores[h] * scale) for h in heads]
    own = [jnp.where(own_mask, jnp.exp(own_scores[h] * scale), 0.0) for h in heads]
    total = [
        jnp.sum(weights[h] + others[h], axis=-1, keepdims=True) + jnp.sum(own[h], axis=-1, keepdims=True)
        for h in heads
    ]
    attended = [
        jnp.dot(weights[h].astype(jnp.bfloat16), kv_ref[:, vcols[h]], preferred_element_type=jnp.float32)
        + jnp.dot(others[h].astype(jnp.bfloat16), other_ref[:, vcols[h]], preferred_element_type=jnp.float32)
        + jnp.dot(own[h].astype(jnp.bfloat16), value[h], preferred_element_type=jnp.float32)
        for h in heads
    ]
    for h in heads:
        state = near_ref[member % 2, :, cols[h]].astype(jnp.float32) + gate_ref[0:1, cols[h]] * (attended[h] / total[h])
        state_ref[:, cols[h]] = state.astype(jnp.bfloat16)
        fresh_ref[:, cols[h]] = key[h]
        fresh_ref[:, vcols[h]] = value[h]


def run_block(tick, who, near, far, weight, kv, other, mod, gate, cosine, sine, blocks, old):
    vmem = pl.BlockSpec(memory_space=pltpu.VMEM)
    weight = pltpu.with_memory_space_constraint(weight, pltpu.VMEM)
    return pl.pallas_call(
        functools.partial(block_kernel, tick),
        out_shape=(
            jax.ShapeDtypeStruct((GROUP, PART), jnp.bfloat16),
            jax.ShapeDtypeStruct((GROUP, 2 * PART), jnp.bfloat16),
        ),
        in_specs=[pl.BlockSpec(memory_space=pltpu.SMEM)] + [vmem] * 11,
        out_specs=(vmem, vmem),
        compiler_params=pltpu.CompilerParams(vmem_limit_bytes=8 * 1024 * 1024),
        name="block_step",
    )(who, near, far, weight, kv, other, mod, gate, cosine, sine, blocks, old)


def prepare_kernel(where, stale_ref, columns_ref, out_ref, half_ref):
    for slot in range(2 * 4 * 2):
        m = slot // 8 * 2 + slot % 2
        out_ref[slot, :, :PART] = stale_ref[:, m * PART : (m + 1) * PART]
        out_ref[slot, :, PART:] = stale_ref[:, D + m * PART : D + (m + 1) * PART]
    half_ref[...] = columns_ref[:, pl.ds(pl.multiple_of(where[3] % 2 * HALF, 128), HALF)]


def pick_kernel(where, x_ref, keep_ref, send_ref):
    member, first, core = where[0], where[1], where[2]
    peer = member + 1 - 2 * core
    for j in range(UNITS):
        third = (first + j * UNIT) // PART
        keep_ref[j * UNIT : (j + 1) * UNIT, :] = x_ref[(third - member + 4) % 4, j * UNIT : (j + 1) * UNIT, :]
        send_ref[j * UNIT : (j + 1) * UNIT, :] = x_ref[(third - peer + 4) % 4, j * UNIT : (j + 1) * UNIT, :]


def place_kernel(where, own, up1, up2, up3, down1, down2, down3, up4, down4, out_ref, rows, sem):
    member, core, y = where[0], where[2], where[3]
    sign = 1 - 2 * core
    copies = []

    def home(unit):
        third = unit // 8
        part = (COLUMNS * 8 * ((third - member + 4) % 4) + PART * third) // D
        return part * PART + unit % 8 * UNIT

    def put(source, part, ref, begin):
        at = (y + sign * source + 8) % 8
        first = (at // 2 * 2 + (core + part) % 2) * UNITS
        for j in range(UNITS):
            unit = first + j
            row = pl.multiple_of(home(unit), 16)
            col = pl.multiple_of(at % 2 * HALF, 128)
            copy = pltpu.make_async_copy(
                ref.at[pl.ds(begin + j * UNIT, UNIT)], rows.at[pl.ds(row, UNIT), pl.ds(col, HALF)], sem
            )
            copy.start()
            copies.append(copy)

    for source, ref in ((0, own), (-1, up1), (-2, up2), (-3, up3), (1, down1), (2, down2), (3, down3)):
        put(source, 0, ref, 0)
        put(source, 1, ref, COLUMNS)
    put(4, 0, up4, 0)
    put(4, 1, down4, 0)
    for copy in copies:
        copy.wait()
    for c in range(0, D, HDIM):
        out_ref[c : c + HDIM, :] = jnp.transpose(rows[:, c : c + HDIM])


def place(where, blocks):
    return pl.pallas_call(
        place_kernel,
        out_shape=jax.ShapeDtypeStruct((D, 3 * PART), jnp.bfloat16),
        in_specs=[pl.BlockSpec(memory_space=pltpu.SMEM)] + [pl.BlockSpec(memory_space=pl.ANY)] * len(blocks),
        out_specs=pl.BlockSpec(memory_space=pltpu.VMEM),
        scratch_shapes=[pltpu.VMEM((3 * PART, D), jnp.bfloat16), pltpu.SemaphoreType.DMA],
        compiler_params=pltpu.CompilerParams(vmem_limit_bytes=8 * 1024 * 1024),
        name="place_weight",
    )(where, *blocks)


def whole_call(kernel, where, arrays, outs):
    vmem = pl.BlockSpec(memory_space=pltpu.VMEM)
    return pl.pallas_call(
        kernel,
        out_shape=[jax.ShapeDtypeStruct(shape, jnp.bfloat16) for shape in outs],
        in_specs=[pl.BlockSpec(memory_space=pltpu.SMEM)] + [vmem] * len(arrays),
        out_specs=[vmem] * len(outs),
        compiler_params=pltpu.CompilerParams(vmem_limit_bytes=8 * 1024 * 1024),
        name=kernel.__name__,
    )(where, *arrays)


def body(hidden, timestep, patch_order, modulation, qkv_weight, stale_kv):
    index = {a: lax.axis_index(a) for a in AXES}
    section = index["section"]
    member = index["xl"] * 2 + index["core"]
    y = index["yh"] * 2 + index["cfg"]
    first = (index["yh"] * 2 + index["core"]) * COLUMNS
    where = jnp.stack([member, first, index["core"], y]).astype(jnp.int32)
    who = jnp.stack([member, section]).astype(jnp.int32)

    outgoing, columns = whole_call(
        prepare_kernel,
        where,
        [stale_kv[0, 0], jnp.transpose(qkv_weight[0])],
        [(2 * 4 * 2, LOCAL, 2 * PART), (COLUMNS, HALF)],
    )
    kv = lax.all_to_all(outgoing, ("xl", "yh", "core"), split_axis=0, concat_axis=0, tiled=True)
    kv = kv.reshape(TOKENS // 2, 2 * PART)

    columns = lax.all_gather(columns, ("xh", "xl"), axis=0, tiled=False)
    keep, send = whole_call(pick_kernel, where, [columns], [(COLUMNS, HALF)] * 2)
    own = jnp.concatenate([keep, lax.ppermute(send, AXES, SWAP)])
    own, kv = lax.optimization_barrier((own, kv))
    up1, down1 = lax.ppermute(own, AXES, UP), lax.ppermute(own, AXES, DOWN)
    up1, entering, kv = lax.optimization_barrier((up1, hidden[0], kv))
    kv_other = lax.ppermute(kv, AXES, ACROSS)
    x = lax.all_gather(entering, ("xl", "core"), axis=0, tiled=True)
    up2, down2 = lax.ppermute(up1, AXES, UP), lax.ppermute(down1, AXES, DOWN)
    down2, x = lax.optimization_barrier((down2, x))
    up3, down3 = lax.ppermute(up2, AXES, UP), lax.ppermute(down2, AXES, DOWN)
    up4 = lax.ppermute(up3[:COLUMNS], AXES, UP)
    down4 = lax.ppermute(down3[COLUMNS:], AXES, DOWN)
    weight = place(where, [own, up1, up2, up3, down1, down2, down3, up4, down4])
    x = jnp.transpose(x.reshape(GROUP, MEMBERS, PART), (1, 0, 2))
    near = lax.dynamic_slice_in_dim(x, index["xl"] * 2, 2, 0)
    far = lax.dynamic_slice_in_dim(x, 2 - index["xl"] * 2, 2, 0)

    row = lax.dynamic_index_in_dim(modulation[0, 0], timestep[0], 0, keepdims=False)
    mod = row[: 2 * D].reshape(2, D)
    gate = lax.dynamic_slice_in_dim(row, 2 * D + member * PART, PART, 0).reshape(1, PART)

    lane = jnp.arange(GROUP, dtype=jnp.int32)
    source = lane // LOCAL
    patch = (source // 2 * 4 + index["yh"]) * 2 + source % 2
    blocks = patch * (LOCAL // ROWS) + lane % LOCAL // ROWS
    positions = (patch_order[index["xh"] * (TOKENS // 2 // ROWS) + blocks] * ROWS + lane % ROWS).astype(jnp.float32)
    halfway = HDIM // 2
    inverse = jnp.exp(-math.log(10000.0) * jnp.arange(halfway, dtype=jnp.float32) / halfway)
    angles = positions[:, None] * inverse[None, :]
    cosine, sine = jnp.cos(angles), jnp.sin(angles)
    cosine = jnp.concatenate([cosine, cosine], axis=1)
    sine = jnp.concatenate([-sine, sine], axis=1)

    fresh = jnp.zeros((GROUP, 2 * PART), jnp.bfloat16)
    for tick in range(SECTIONS):
        state, fresh = run_block(tick, who, near, far, weight, kv, kv_other, mod, gate, cosine, sine, blocks[:, None], fresh)
        if tick + 1 < SECTIONS:
            near = lax.ppermute(state, AXES, onward(tick, 0))
            far = lax.ppermute(state, AXES, onward(tick, 1))
            near = lax.all_gather(near, "core", axis=0, tiled=False)
            far = lax.all_gather(far, "core", axis=0, tiled=False)

    ends = lax.all_gather(state, ("xl", "core"), axis=0, tiled=False)
    finals = lax.dynamic_slice_in_dim(ends, member * LOCAL, LOCAL, 1)
    finals = jnp.transpose(finals, (1, 0, 2)).reshape(SECTIONS, LOCAL // SECTIONS, 2, D // 2)
    finals = jnp.transpose(finals, (0, 2, 1, 3)).reshape(SECTIONS * 2, LOCAL // SECTIONS, D // 2)
    spread = lax.all_to_all(finals, ("section", "cfg"), split_axis=0, concat_axis=0, tiled=True)
    kept = lax.all_gather(fresh, ("xl", "core"), axis=0, tiled=False)
    spread, kept = lax.optimization_barrier((spread, kept))
    kept = lax.dynamic_slice_in_dim(kept, member * LOCAL, LOCAL, 1)
    kept = jnp.transpose(kept.reshape(MEMBERS, LOCAL, 2, PART), (1, 2, 0, 3)).reshape(LOCAL, 2 * D)
    uncond = spread[2 * SECTIONS - 2].astype(jnp.float32)
    conditioned = spread[2 * SECTIONS - 1].astype(jnp.float32)
    guided = (uncond + guide_weight * (conditioned - uncond)).astype(jnp.bfloat16)
    return guided, kept[None, None]


def solution(mesh):
    fine = Mesh(mesh.devices.reshape(SIZES), AXES)
    patch = ("xh", "xl", "yh", "core")
    return jax.shard_map(
        body,
        mesh=fine,
        in_specs=(
            P("cfg", patch, None),
            P(),
            P(),
            P("section", "cfg", None, None),
            P("section", None, patch),
            P("section", "cfg", patch, None),
        ),
        out_specs=(P((*patch, "section"), "cfg"), P("section", "cfg", patch, None)),
        check_vma=False,
    )
```

```python
import functools
import math

import jax
import jax.numpy as jnp
import numpy as np
from jax import lax
from jax.experimental import pallas as pl
from jax.experimental.pallas import tpu as pltpu
from jax.sharding import Mesh, PartitionSpec as P

HEADS = 12
HDIM = 128
ROWS = 8
D = HEADS * HDIM
TOKENS = 512
SECTIONS = 8
MEMBERS = 4
PART = D // MEMBERS
LOCAL = 16
GROUP = LOCAL * MEMBERS
UNIT = 48
UNITS = 3
COLUMNS = UNIT * UNITS
HALF = D // 2
BLOCK = 2 * COLUMNS

guide_weight = 3.5
norm_eps = 1e-06

AXES = ("xh", "xl", "yh", "core", "section", "cfg")
SIZES = (2, 2, 4, 2, 8, 2)


def route(step):
    def number(x, y, core, section):
        return (((x * 4 + y // 2) * 2 + core) * 8 + section) * 2 + y % 2

    return [
        (number(x, y, core, s), number(*step(x, y, core), s))
        for x in range(4)
        for y in range(8)
        for core in range(2)
        for s in range(SECTIONS)
    ]


def member_at(x, y, core, row):
    return (((y // 2 * 2 + core) * COLUMNS + row) // PART - x) % 4


def spread(copy, row):
    def step(x, y, core):
        member = member_at(x, y, core, row(y, core))
        return (copy(core) * 2 + member // 2, y, member % 2)

    return route(step)


def cut(y, core):
    if (y // 2, core) == (1, 0):
        return 1, 2 * UNIT, 0
    if (y // 2, core) == (2, 1):
        return 1, 0, UNIT
    return 0, 0, 0


MAIN = [spread(lambda core, k=k: core ^ k, lambda y, core: cut(y, core)[2]) for k in range(2)]
TURN = [spread(lambda core, k=k: k, lambda y, core: cut(y, core)[1]) for k in range(2)]
_CUTS = {n for n in range(512) if cut(n // 16 // 2 % 4 * 2 + n % 2, n // 16 % 2)[0]}
TURN = [[edge for edge in edges if edge[0] in _CUTS] for edges in TURN]
UP = route(lambda x, y, core: (x, (y + 1 - 2 * core) % 8, core))
DOWN = route(lambda x, y, core: (x, (y - 1 + 2 * core) % 8, core))
ACROSS = [(i, (i + 256) % 512) for i in range(512)]


def onward(section, flip, turn):
    def number(x, y, core, s):
        return (((x * 4 + y // 2) * 2 + core) * 8 + s) * 2 + y % 2

    return [
        (number(x, y, core, section), number(x ^ flip, y, core ^ turn, section + 1))
        for x in range(4)
        for y in range(8)
        for core in range(2)
    ]


def nt_dot(a, b):
    return lax.dot_general(a, b, (((1,), (1,)), ((), ())), preferred_element_type=jnp.float32)


def block_kernel(tick, who, near_ref, cross_ref, far_ref, w_ref, kv_ref, other_ref, mod_ref, gate_ref, cos_ref, sin_ref, block_ref, old_ref, state_ref, fresh_ref):
    active = who[1] == tick

    @pl.when(jnp.logical_not(active))
    def _():
        fresh_ref[...] = old_ref[...]

    @pl.when(active)
    def _():
        active_block(who[0], near_ref, cross_ref, far_ref, w_ref, kv_ref, other_ref, mod_ref, gate_ref, cos_ref, sin_ref, block_ref, state_ref, fresh_ref)


def active_block(member, near_ref, cross_ref, far_ref, w_ref, kv_ref, other_ref, mod_ref, gate_ref, cos_ref, sin_ref, block_ref, state_ref, fresh_ref):
    near, cross = near_ref[...].astype(jnp.float32), cross_ref[...].astype(jnp.float32)
    first = member % 2 == 0
    near = [jnp.where(first, near, cross), jnp.where(first, cross, near)]
    far = [far_ref[core].astype(jnp.float32) for core in range(2)]
    low = member < 2
    xs = [jnp.where(low, near[core], far[core]) for core in range(2)]
    xs += [jnp.where(low, far[core], near[core]) for core in range(2)]
    center = sum(jnp.sum(x, axis=-1, keepdims=True) for x in xs) / D
    xs = [x - center for x in xs]
    spread = sum(jnp.sum(x * x, axis=-1, keepdims=True) for x in xs) / D
    inv = lax.rsqrt(spread + norm_eps)
    normed = jnp.concatenate(
        [
            (
                xs[i] * inv * (1.0 + mod_ref[1:2, i * PART : (i + 1) * PART])
                + mod_ref[0:1, i * PART : (i + 1) * PART]
            ).astype(jnp.bfloat16)
            for i in range(MEMBERS)
        ],
        axis=1,
    )
    projected = jnp.dot(normed, w_ref[...], preferred_element_type=jnp.float32).astype(jnp.bfloat16)
    row_block = block_ref[...]
    stale_mask = lax.broadcasted_iota(jnp.int32, (GROUP, TOKENS // 2), 1) // ROWS == row_block
    own_mask = (
        lax.broadcasted_iota(jnp.int32, (GROUP, GROUP), 0) // ROWS
        == lax.broadcasted_iota(jnp.int32, (GROUP, GROUP), 1) // ROWS
    )
    cosine, sine = cos_ref[...], sin_ref[...]

    def turned(values):
        values = values.astype(jnp.float32)
        values = values * lax.rsqrt(jnp.mean(values * values, axis=-1, keepdims=True) + norm_eps)
        return (values * cosine + pltpu.roll(values, HDIM // 2, 1) * sine).astype(jnp.bfloat16)

    heads = range(PART // HDIM)
    cols = [slice(h * HDIM, (h + 1) * HDIM) for h in heads]
    vcols = [slice(PART + h * HDIM, PART + (h + 1) * HDIM) for h in heads]
    scale = 1.0 / math.sqrt(HDIM)
    query = [turned(projected[:, cols[h]]) for h in heads]
    key = [turned(projected[:, vcols[h]]) for h in heads]
    value = [projected[:, 2 * PART + h * HDIM : 2 * PART + (h + 1) * HDIM] for h in heads]
    scores = [nt_dot(query[h], kv_ref[:, cols[h]]) for h in heads]
    other_scores = [nt_dot(query[h], other_ref[:, cols[h]]) for h in heads]
    own_scores = [nt_dot(query[h], key[h]) for h in heads]
    weights = [jnp.where(stale_mask, 0.0, jnp.exp(scores[h] * scale)) for h in heads]
    others = [jnp.exp(other_scores[h] * scale) for h in heads]
    own = [jnp.where(own_mask, jnp.exp(own_scores[h] * scale), 0.0) for h in heads]
    total = [
        jnp.sum(weights[h] + others[h], axis=-1, keepdims=True) + jnp.sum(own[h], axis=-1, keepdims=True)
        for h in heads
    ]
    attended = [
        jnp.dot(weights[h].astype(jnp.bfloat16), kv_ref[:, vcols[h]], preferred_element_type=jnp.float32)
        + jnp.dot(others[h].astype(jnp.bfloat16), other_ref[:, vcols[h]], preferred_element_type=jnp.float32)
        + jnp.dot(own[h].astype(jnp.bfloat16), value[h], preferred_element_type=jnp.float32)
        for h in heads
    ]
    for h in heads:
        state = near_ref[:, cols[h]].astype(jnp.float32) + gate_ref[0:1, cols[h]] * (attended[h] / total[h])
        state_ref[:, cols[h]] = state.astype(jnp.bfloat16)
        fresh_ref[:, cols[h]] = key[h]
        fresh_ref[:, vcols[h]] = value[h]


def run_block(tick, who, near, cross, far, weight, kv, other, mod, gate, cosine, sine, blocks, old):
    vmem = pl.BlockSpec(memory_space=pltpu.VMEM)
    weight = pltpu.with_memory_space_constraint(weight, pltpu.VMEM)
    return pl.pallas_call(
        functools.partial(block_kernel, tick),
        out_shape=(
            jax.ShapeDtypeStruct((GROUP, PART), jnp.bfloat16),
            jax.ShapeDtypeStruct((GROUP, 2 * PART), jnp.bfloat16),
        ),
        in_specs=[pl.BlockSpec(memory_space=pltpu.SMEM)] + [vmem] * 12,
        out_specs=(vmem, vmem),
        compiler_params=pltpu.CompilerParams(vmem_limit_bytes=8 * 1024 * 1024),
        name="block_step",
    )(who, near, cross, far, weight, kv, other, mod, gate, cosine, sine, blocks, old)


def half_kernel(where, columns_ref, half_ref, turn_ref, sems):
    first = jnp.where(where[2] == 0, 2 * UNIT, 0)
    col = pl.ds(pl.multiple_of(where[3] % 2 * HALF, 128), HALF)
    whole = pltpu.make_async_copy(columns_ref.at[:, col], half_ref, sems.at[0])
    turn = pltpu.make_async_copy(
        columns_ref.at[pl.ds(pl.multiple_of(first, 16), UNIT), col], turn_ref, sems.at[1]
    )
    whole.start()
    turn.start()
    whole.wait()
    turn.wait()


def stale_kernel(where, stale_ref, out_ref, sem):
    copies = []
    for slot in range(2 * 4 * 2):
        m = slot // 8 * 2 + slot % 2
        for part in range(2):
            copies.append(
                pltpu.make_async_copy(
                    stale_ref.at[:, part * D + m * PART : part * D + (m + 1) * PART],
                    out_ref.at[slot, :, part * PART : (part + 1) * PART],
                    sem,
                )
            )
            copies[-1].start()
    for copy in copies:
        copy.wait()


def join_kernel(where, first_ref, second_ref, turn0_ref, turn1_ref, own_ref):
    half, y = where[1], where[3]

    def pick(one, two):
        return jnp.where(half == 0, one[...], two[...])

    own_ref[:COLUMNS, :] = pick(first_ref, second_ref)
    own_ref[COLUMNS:, :] = pick(second_ref, first_ref)

    @pl.when(y // 2 == 1)
    def _():
        own_ref[2 * UNIT : COLUMNS, :] = pick(turn0_ref, turn1_ref)

    @pl.when(y // 2 == 2)
    def _():
        own_ref[COLUMNS : COLUMNS + UNIT, :] = pick(turn0_ref, turn1_ref)


def place_kernel(sources, last, where, *refs):
    blocks, refs = refs[: len(sources)], refs[len(sources) :]
    rows, sem = (refs[1], refs[3]) if last else (refs[0], refs[1])
    member, core, y = where[0], where[2], where[3]
    sign = 1 - 2 * core
    copies = []

    def home(unit):
        third = unit // 8
        part = (COLUMNS * 8 * ((third - member + 4) % 4) + PART * third) // D
        return part * PART + unit % 8 * UNIT

    for (source, parts), ref in zip(sources, blocks):
        at = (y + sign * source + 8) % 8
        col = pl.ds(pl.multiple_of(at % 2 * HALF, 128), HALF)
        for n, part in enumerate(parts):
            for j in range(UNITS):
                row = pl.multiple_of(home((at // 2 * 2 + part) * UNITS + j), 16)
                copy = pltpu.make_async_copy(
                    ref.at[pl.ds(n * COLUMNS + j * UNIT, UNIT)], rows.at[pl.ds(row, UNIT), col], sem
                )
                copy.start()
                copies.append(copy)
    for copy in copies:
        copy.wait()
    if last:
        for c in range(0, D, HDIM):
            refs[2][c : c + HDIM, :] = jnp.transpose(rows[:, c : c + HDIM])


def place(sources, where, blocks, rows=None):
    last = rows is not None
    held = pl.BlockSpec(memory_space=pl.ANY)
    vmem = pl.BlockSpec(memory_space=pltpu.VMEM)
    whole = jax.ShapeDtypeStruct((3 * PART, D), jnp.bfloat16)
    turned = jax.ShapeDtypeStruct((D, 3 * PART), jnp.bfloat16)
    return pl.pallas_call(
        functools.partial(place_kernel, sources, last),
        out_shape=(whole, turned) if last else whole,
        in_specs=[pl.BlockSpec(memory_space=pltpu.SMEM)] + [held] * len(blocks) + [vmem] * last,
        out_specs=(vmem, vmem) if last else vmem,
        input_output_aliases={len(blocks) + 1: 0} if last else {},
        scratch_shapes=[pltpu.SemaphoreType.DMA],
        compiler_params=pltpu.CompilerParams(vmem_limit_bytes=12 * 1024 * 1024),
        name="place_last" if last else "place_first",
    )(where, *blocks, *([rows] if last else []))


def whole_call(kernel, where, arrays, outs, sems=()):
    vmem = pl.BlockSpec(memory_space=pltpu.VMEM)
    held = pl.BlockSpec(memory_space=pl.ANY) if sems else vmem
    return pl.pallas_call(
        kernel,
        out_shape=[jax.ShapeDtypeStruct(shape, jnp.bfloat16) for shape in outs],
        in_specs=[pl.BlockSpec(memory_space=pltpu.SMEM)] + [held] * len(arrays),
        out_specs=[vmem] * len(outs),
        scratch_shapes=list(sems),
        compiler_params=pltpu.CompilerParams(vmem_limit_bytes=8 * 1024 * 1024),
        name=kernel.__name__,
    )(where, *arrays)


def body(hidden, timestep, patch_order, modulation, qkv_weight, stale_kv):
    index = {a: lax.axis_index(a) for a in AXES}
    section = index["section"]
    member = index["xl"] * 2 + index["core"]
    y = index["yh"] * 2 + index["cfg"]
    where = jnp.stack([member, index["xh"], index["core"], y]).astype(jnp.int32)
    who = jnp.stack([member, section]).astype(jnp.int32)

    half, turn = whole_call(
        half_kernel,
        where,
        [jnp.transpose(qkv_weight[0])],
        [(COLUMNS, HALF), (UNIT, HALF)],
        [pltpu.SemaphoreType.DMA((2,))],
    )
    moved = [lax.ppermute(half, AXES, edges) for edges in MAIN]
    turned = [lax.ppermute(turn, AXES, edges) for edges in TURN]
    (outgoing,) = whole_call(
        stale_kernel, where, [stale_kv[0, 0]], [(2 * 4 * 2, LOCAL, 2 * PART)], [pltpu.SemaphoreType.DMA]
    )
    kv = lax.all_to_all(outgoing, ("xl", "yh", "core"), split_axis=0, concat_axis=0, tiled=True)
    kv = kv.reshape(TOKENS // 2, 2 * PART)
    (own,) = whole_call(join_kernel, where, [*moved, *turned], [(BLOCK, HALF)])
    up1, down1 = lax.ppermute(own, AXES, UP), lax.ppermute(own, AXES, DOWN)
    up1, entering, kv = lax.optimization_barrier((up1, hidden[0], kv))
    kv_other = lax.ppermute(kv, AXES, ACROSS)
    x = lax.all_gather(entering, ("xl", "core"), axis=0, tiled=True)
    up2, down2 = lax.ppermute(up1, AXES, UP), lax.ppermute(down1, AXES, DOWN)
    down2, x = lax.optimization_barrier((down2, x))
    up3, down3 = lax.ppermute(up2, AXES, UP), lax.ppermute(down2, AXES, DOWN)
    up4 = lax.ppermute(up3[:COLUMNS], AXES, UP)
    down4 = lax.ppermute(down3[COLUMNS:], AXES, DOWN)
    both = (0, 1)
    rows = place(
        ((0, both), (-1, both), (1, both), (-2, both), (2, both)), where, [own, up1, down1, up2, down2]
    )
    _, weight = place(((-3, both), (3, both), (4, (0,)), (4, (1,))), where, [up3, down3, up4, down4], rows)
    x = jnp.transpose(x.reshape(GROUP, MEMBERS, PART), (1, 0, 2))
    near = lax.dynamic_index_in_dim(x, member, 0, keepdims=False)
    cross = lax.dynamic_index_in_dim(x, member + 1 - 2 * index["core"], 0, keepdims=False)
    far = lax.dynamic_slice_in_dim(x, 2 - index["xl"] * 2, 2, 0)

    row = lax.dynamic_index_in_dim(modulation[0, 0], timestep[0], 0, keepdims=False)
    mod = row[: 2 * D].reshape(2, D)
    gate = lax.dynamic_slice_in_dim(row, 2 * D + member * PART, PART, 0).reshape(1, PART)

    lane = jnp.arange(GROUP, dtype=jnp.int32)
    source = lane // LOCAL
    patch = (source // 2 * 4 + index["yh"]) * 2 + source % 2
    blocks = patch * (LOCAL // ROWS) + lane % LOCAL // ROWS
    positions = (patch_order[index["xh"] * (TOKENS // 2 // ROWS) + blocks] * ROWS + lane % ROWS).astype(jnp.float32)
    halfway = HDIM // 2
    inverse = jnp.exp(-math.log(10000.0) * jnp.arange(halfway, dtype=jnp.float32) / halfway)
    angles = positions[:, None] * inverse[None, :]
    cosine, sine = jnp.cos(angles), jnp.sin(angles)
    cosine = jnp.concatenate([cosine, cosine], axis=1)
    sine = jnp.concatenate([-sine, sine], axis=1)

    fresh = jnp.zeros((GROUP, 2 * PART), jnp.bfloat16)
    for tick in range(SECTIONS):
        state, fresh = run_block(tick, who, near, cross, far, weight, kv, kv_other, mod, gate, cosine, sine, blocks[:, None], fresh)
        if tick + 1 < SECTIONS:
            far = lax.ppermute(state, AXES, onward(tick, 1, 0))
            near = lax.ppermute(state, AXES, onward(tick, 0, 0))
            cross = lax.ppermute(state, AXES, onward(tick, 0, 1))
            far = lax.all_gather(far, "core", axis=0, tiled=False)

    ends = lax.all_gather(state, ("xl", "core"), axis=0, tiled=False)
    finals = lax.dynamic_slice_in_dim(ends, member * LOCAL, LOCAL, 1)
    finals = jnp.transpose(finals, (1, 0, 2)).reshape(SECTIONS, LOCAL // SECTIONS, 2, D // 2)
    finals = jnp.transpose(finals, (0, 2, 1, 3)).reshape(SECTIONS * 2, LOCAL // SECTIONS, D // 2)
    spread = lax.all_to_all(finals, ("section", "cfg"), split_axis=0, concat_axis=0, tiled=True)
    kept = lax.all_gather(fresh, ("xl", "core"), axis=0, tiled=False)
    spread, kept = lax.optimization_barrier((spread, kept))
    kept = lax.dynamic_slice_in_dim(kept, member * LOCAL, LOCAL, 1)
    kept = jnp.transpose(kept.reshape(MEMBERS, LOCAL, 2, PART), (1, 2, 0, 3)).reshape(LOCAL, 2 * D)
    uncond = spread[2 * SECTIONS - 2].astype(jnp.float32)
    conditioned = spread[2 * SECTIONS - 1].astype(jnp.float32)
    guided = (uncond + guide_weight * (conditioned - uncond)).astype(jnp.bfloat16)
    return guided, kept[None, None]


def solution(mesh):
    fine = Mesh(mesh.devices.reshape(SIZES), AXES)
    patch = ("xh", "xl", "yh", "core")
    return jax.shard_map(
        body,
        mesh=fine,
        in_specs=(
            P("cfg", patch, None),
            P(),
            P(),
            P("section", "cfg", None, None),
            P("section", None, patch),
            P("section", "cfg", patch, None),
        ),
        out_specs=(P((*patch, "section"), "cfg"), P("section", "cfg", patch, None)),
        check_vma=False,
    )
```

```python
import functools
import math

import jax
import jax.numpy as jnp
import numpy as np
from jax import lax
from jax.experimental import pallas as pl
from jax.experimental.pallas import tpu as pltpu
from jax.sharding import Mesh, PartitionSpec as P

HEADS = 12
HDIM = 128
ROWS = 8
D = HEADS * HDIM
TOKENS = 512
SECTIONS = 8
MEMBERS = 4
PART = D // MEMBERS
LOCAL = 16
GROUP = LOCAL * MEMBERS
UNIT = 48
UNITS = 3
COLUMNS = UNIT * UNITS
HALF = D // 2
BLOCK = 2 * COLUMNS

guide_weight = 3.5
norm_eps = 1e-06

AXES = ("xh", "xl", "yh", "core", "section", "cfg")
SIZES = (2, 2, 4, 2, 8, 2)


def route(step):
    def number(x, y, core, section):
        return (((x * 4 + y // 2) * 2 + core) * 8 + section) * 2 + y % 2

    return [
        (number(x, y, core, s), number(*step(x, y, core), s))
        for x in range(4)
        for y in range(8)
        for core in range(2)
        for s in range(SECTIONS)
    ]


def member_at(x, y, core, row):
    return (((y // 2 * 2 + core) * COLUMNS + row) // PART - x) % 4


def spread(copy, row):
    def step(x, y, core):
        member = member_at(x, y, core, row(y, core))
        return (copy(core) * 2 + member // 2, y, member % 2)

    return route(step)


def cut(y, core):
    if (y // 2, core) == (1, 0):
        return 1, 2 * UNIT, 0
    if (y // 2, core) == (2, 1):
        return 1, 0, UNIT
    return 0, 0, 0


MAIN = [spread(lambda core, k=k: core ^ k, lambda y, core: cut(y, core)[2]) for k in range(2)]
TURN = [spread(lambda core, k=k: k, lambda y, core: cut(y, core)[1]) for k in range(2)]
_CUTS = {n for n in range(512) if cut(n // 16 // 2 % 4 * 2 + n % 2, n // 16 % 2)[0]}
TURN = [[edge for edge in edges if edge[0] in _CUTS] for edges in TURN]
UP = route(lambda x, y, core: (x, (y + 1 - 2 * core) % 8, core))
DOWN = route(lambda x, y, core: (x, (y - 1 + 2 * core) % 8, core))
ACROSS = [(i, (i + 256) % 512) for i in range(512)]


def place_of(x, y, core, section):
    return (((x * 4 + y // 2) * 2 + core) * 8 + section) * 2 + y % 2


PLANE = [(x, y, core) for x in range(4) for y in range(8) for core in range(2)]
LAST = SECTIONS - 1


def onward(tick, flip, turn):
    return [
        (place_of(x, y, core, section), place_of(x ^ flip, y, core ^ turn, section + 1))
        for section in range(tick % 4, LAST, 4)
        for x, y, core in PLANE
    ]


def nt_dot(a, b):
    return lax.dot_general(a, b, (((1,), (1,)), ((), ())), preferred_element_type=jnp.float32)


def block_kernel(tick, who, near_ref, cross_ref, far_ref, w_ref, kv_ref, other_ref, mod_ref, gate_ref, cos_ref, sin_ref, block_ref, old_ref, state_ref, fresh_ref):
    active = who[1] == tick

    @pl.when(jnp.logical_not(active))
    def _():
        fresh_ref[...] = old_ref[...]

    @pl.when(active)
    def _():
        active_block(who[0], near_ref, cross_ref, far_ref, w_ref, kv_ref, other_ref, mod_ref, gate_ref, cos_ref, sin_ref, block_ref, state_ref, fresh_ref)


def active_block(member, near_ref, cross_ref, far_ref, w_ref, kv_ref, other_ref, mod_ref, gate_ref, cos_ref, sin_ref, block_ref, state_ref, fresh_ref):
    near, cross = near_ref[...].astype(jnp.float32), cross_ref[...].astype(jnp.float32)
    first = member % 2 == 0
    near = [jnp.where(first, near, cross), jnp.where(first, cross, near)]
    far = [far_ref[core].astype(jnp.float32) for core in range(2)]
    low = member < 2
    xs = [jnp.where(low, near[core], far[core]) for core in range(2)]
    xs += [jnp.where(low, far[core], near[core]) for core in range(2)]
    center = sum(jnp.sum(x, axis=-1, keepdims=True) for x in xs) / D
    xs = [x - center for x in xs]
    spread = sum(jnp.sum(x * x, axis=-1, keepdims=True) for x in xs) / D
    inv = lax.rsqrt(spread + norm_eps)
    normed = jnp.concatenate(
        [
            (
                xs[i] * inv * (1.0 + mod_ref[1:2, i * PART : (i + 1) * PART])
                + mod_ref[0:1, i * PART : (i + 1) * PART]
            ).astype(jnp.bfloat16)
            for i in range(MEMBERS)
        ],
        axis=1,
    )
    projected = jnp.dot(normed, w_ref[...], preferred_element_type=jnp.float32).astype(jnp.bfloat16)
    row_block = block_ref[...]
    stale_mask = lax.broadcasted_iota(jnp.int32, (GROUP, TOKENS // 2), 1) // ROWS == row_block
    own_mask = (
        lax.broadcasted_iota(jnp.int32, (GROUP, GROUP), 0) // ROWS
        == lax.broadcasted_iota(jnp.int32, (GROUP, GROUP), 1) // ROWS
    )
    cosine, sine = cos_ref[...], sin_ref[...]

    def turned(values):
        values = values.astype(jnp.float32)
        values = values * lax.rsqrt(jnp.mean(values * values, axis=-1, keepdims=True) + norm_eps)
        return (values * cosine + pltpu.roll(values, HDIM // 2, 1) * sine).astype(jnp.bfloat16)

    heads = range(PART // HDIM)
    cols = [slice(h * HDIM, (h + 1) * HDIM) for h in heads]
    vcols = [slice(PART + h * HDIM, PART + (h + 1) * HDIM) for h in heads]
    scale = 1.0 / math.sqrt(HDIM)
    query = [turned(projected[:, cols[h]]) for h in heads]
    key = [turned(projected[:, vcols[h]]) for h in heads]
    value = [projected[:, 2 * PART + h * HDIM : 2 * PART + (h + 1) * HDIM] for h in heads]
    scores = [nt_dot(query[h], kv_ref[:, cols[h]]) for h in heads]
    other_scores = [nt_dot(query[h], other_ref[:, cols[h]]) for h in heads]
    own_scores = [nt_dot(query[h], key[h]) for h in heads]
    weights = [jnp.where(stale_mask, 0.0, jnp.exp(scores[h] * scale)) for h in heads]
    others = [jnp.exp(other_scores[h] * scale) for h in heads]
    own = [jnp.where(own_mask, jnp.exp(own_scores[h] * scale), 0.0) for h in heads]
    total = [
        jnp.sum(weights[h] + others[h], axis=-1, keepdims=True) + jnp.sum(own[h], axis=-1, keepdims=True)
        for h in heads
    ]
    attended = [
        jnp.dot(weights[h].astype(jnp.bfloat16), kv_ref[:, vcols[h]], preferred_element_type=jnp.float32)
        + jnp.dot(others[h].astype(jnp.bfloat16), other_ref[:, vcols[h]], preferred_element_type=jnp.float32)
        + jnp.dot(own[h].astype(jnp.bfloat16), value[h], preferred_element_type=jnp.float32)
        for h in heads
    ]
    for h in heads:
        state = near_ref[:, cols[h]].astype(jnp.float32) + gate_ref[0:1, cols[h]] * (attended[h] / total[h])
        state_ref[:, cols[h]] = state.astype(jnp.bfloat16)
        fresh_ref[:, cols[h]] = key[h]
        fresh_ref[:, vcols[h]] = value[h]


def run_block(tick, who, near, cross, far, weight, kv, other, mod, gate, cosine, sine, blocks, old):
    vmem = pl.BlockSpec(memory_space=pltpu.VMEM)
    weight = pltpu.with_memory_space_constraint(weight, pltpu.VMEM)
    return pl.pallas_call(
        functools.partial(block_kernel, tick),
        out_shape=(
            jax.ShapeDtypeStruct((GROUP, PART), jnp.bfloat16),
            jax.ShapeDtypeStruct((GROUP, 2 * PART), jnp.bfloat16),
        ),
        in_specs=[pl.BlockSpec(memory_space=pltpu.SMEM)] + [vmem] * 12,
        out_specs=(vmem, vmem),
        compiler_params=pltpu.CompilerParams(vmem_limit_bytes=8 * 1024 * 1024),
        name="block_step",
    )(who, near, cross, far, weight, kv, other, mod, gate, cosine, sine, blocks, old)


def half_kernel(where, columns_ref, half_ref, turn_ref, sems):
    first = jnp.where(where[2] == 0, 2 * UNIT, 0)
    col = pl.ds(pl.multiple_of(where[3] % 2 * HALF, 128), HALF)
    whole = pltpu.make_async_copy(columns_ref.at[:, col], half_ref, sems.at[0])
    turn = pltpu.make_async_copy(
        columns_ref.at[pl.ds(pl.multiple_of(first, 16), UNIT), col], turn_ref, sems.at[1]
    )
    whole.start()
    turn.start()
    whole.wait()
    turn.wait()


def stale_kernel(where, stale_ref, out_ref, sem):
    copies = []
    for slot in range(2 * 4 * 2):
        m = slot // 8 * 2 + slot % 2
        for part in range(2):
            copies.append(
                pltpu.make_async_copy(
                    stale_ref.at[:, part * D + m * PART : part * D + (m + 1) * PART],
                    out_ref.at[slot, :, part * PART : (part + 1) * PART],
                    sem,
                )
            )
            copies[-1].start()
    for copy in copies:
        copy.wait()


def join_kernel(where, first_ref, second_ref, turn0_ref, turn1_ref, own_ref):
    half, y = where[1], where[3]

    def pick(one, two):
        return jnp.where(half == 0, one[...], two[...])

    own_ref[:COLUMNS, :] = pick(first_ref, second_ref)
    own_ref[COLUMNS:, :] = pick(second_ref, first_ref)

    @pl.when(y // 2 == 1)
    def _():
        own_ref[2 * UNIT : COLUMNS, :] = pick(turn0_ref, turn1_ref)

    @pl.when(y // 2 == 2)
    def _():
        own_ref[COLUMNS : COLUMNS + UNIT, :] = pick(turn0_ref, turn1_ref)


def place_kernel(sources, kind, where, *refs):
    blocks, refs = refs[: len(sources)], refs[len(sources) :]
    rows = refs[{"first": 0, "last": 1, "rest": 2}[kind]]
    sem = refs[-1]
    member, core, y, later = where[0], where[2], where[3], where[4]
    sign = 1 - 2 * core

    def home(unit):
        third = unit // 8
        part = (COLUMNS * 8 * ((third - member + 4) % 4) + PART * third) // D
        return part * PART + unit % 8 * UNIT

    @pl.when(later == (1 if kind == "rest" else 0))
    def _():
        copies = []
        for (source, parts), ref in zip(sources, blocks):
            at = (y + sign * source + 8) % 8
            col = pl.ds(pl.multiple_of(at % 2 * HALF, 128), HALF)
            for n, part in enumerate(parts):
                for j in range(UNITS):
                    row = pl.multiple_of(home((at // 2 * 2 + part) * UNITS + j), 16)
                    copy = pltpu.make_async_copy(
                        ref.at[pl.ds(n * COLUMNS + j * UNIT, UNIT)], rows.at[pl.ds(row, UNIT), col], sem
                    )
                    copy.start()
                    copies.append(copy)
        for copy in copies:
            copy.wait()
        if kind != "first":
            out_ref = refs[2 if kind == "last" else 1]
            for c in range(0, D, HDIM):
                out_ref[c : c + HDIM, :] = jnp.transpose(rows[:, c : c + HDIM])


def place(sources, kind, where, blocks, held=()):
    any_space = pl.BlockSpec(memory_space=pl.ANY)
    vmem = pl.BlockSpec(memory_space=pltpu.VMEM)
    whole = jax.ShapeDtypeStruct((3 * PART, D), jnp.bfloat16)
    turned = jax.ShapeDtypeStruct((D, 3 * PART), jnp.bfloat16)
    scratch = [pltpu.SemaphoreType.DMA]
    if kind == "rest":
        scratch = [pltpu.VMEM((3 * PART, D), jnp.bfloat16), *scratch]
    return pl.pallas_call(
        functools.partial(place_kernel, sources, kind),
        out_shape={"first": whole, "last": (whole, turned), "rest": turned}[kind],
        in_specs=[pl.BlockSpec(memory_space=pltpu.SMEM)] + [any_space] * len(blocks) + [vmem] * len(held),
        out_specs=(vmem, vmem) if kind == "last" else vmem,
        input_output_aliases={len(blocks) + 1: 0} if held else {},
        scratch_shapes=scratch,
        compiler_params=pltpu.CompilerParams(vmem_limit_bytes=12 * 1024 * 1024),
        name="place_" + kind,
    )(where, *blocks, *held)


def whole_call(kernel, where, arrays, outs, sems=()):
    vmem = pl.BlockSpec(memory_space=pltpu.VMEM)
    held = pl.BlockSpec(memory_space=pl.ANY) if sems else vmem
    return pl.pallas_call(
        kernel,
        out_shape=[jax.ShapeDtypeStruct(shape, jnp.bfloat16) for shape in outs],
        in_specs=[pl.BlockSpec(memory_space=pltpu.SMEM)] + [held] * len(arrays),
        out_specs=[vmem] * len(outs),
        scratch_shapes=list(sems),
        compiler_params=pltpu.CompilerParams(vmem_limit_bytes=8 * 1024 * 1024),
        name=kernel.__name__,
    )(where, *arrays)


def body(hidden, timestep, patch_order, modulation, qkv_weight, stale_kv):
    index = {a: lax.axis_index(a) for a in AXES}
    section = index["section"]
    member = index["xl"] * 2 + index["core"]
    y = index["yh"] * 2 + index["cfg"]
    where = jnp.stack([member, index["xh"], index["core"], y, jnp.minimum(section, 1)]).astype(jnp.int32)
    who = jnp.stack([member, section]).astype(jnp.int32)

    half, turn = whole_call(
        half_kernel,
        where,
        [jnp.transpose(qkv_weight[0])],
        [(COLUMNS, HALF), (UNIT, HALF)],
        [pltpu.SemaphoreType.DMA((2,))],
    )
    moved = [lax.ppermute(half, AXES, edges) for edges in MAIN]
    turned = [lax.ppermute(turn, AXES, edges) for edges in TURN]
    (outgoing,) = whole_call(
        stale_kernel, where, [stale_kv[0, 0]], [(2 * 4 * 2, LOCAL, 2 * PART)], [pltpu.SemaphoreType.DMA]
    )
    kv = lax.all_to_all(outgoing, ("xl", "yh", "core"), split_axis=0, concat_axis=0, tiled=True)
    kv = kv.reshape(TOKENS // 2, 2 * PART)
    (own,) = whole_call(join_kernel, where, [*moved, *turned], [(BLOCK, HALF)])
    up1, down1 = lax.ppermute(own, AXES, UP), lax.ppermute(own, AXES, DOWN)
    up1, entering, kv = lax.optimization_barrier((up1, hidden[0], kv))
    kv_other = lax.ppermute(kv, AXES, ACROSS)
    x = lax.all_gather(entering, ("xl", "core"), axis=0, tiled=True)
    up2, down2 = lax.ppermute(up1, AXES, UP), lax.ppermute(down1, AXES, DOWN)
    down2, x = lax.optimization_barrier((down2, x))
    up3, down3 = lax.ppermute(up2, AXES, UP), lax.ppermute(down2, AXES, DOWN)
    up4 = lax.ppermute(up3[:COLUMNS], AXES, UP)
    down4 = lax.ppermute(down3[COLUMNS:], AXES, DOWN)
    both = (0, 1)
    early = ((0, both), (-1, both), (1, both), (-2, both), (2, both)), [own, up1, down1, up2, down2]
    late = ((-3, both), (3, both), (4, (0,)), (4, (1,))), [up3, down3, up4, down4]
    rows = place(early[0], "first", where, early[1])
    _, weight = place(late[0], "last", where, late[1], [rows])
    x = jnp.transpose(x.reshape(GROUP, MEMBERS, PART), (1, 0, 2))
    near = lax.dynamic_index_in_dim(x, member, 0, keepdims=False)
    cross = lax.dynamic_index_in_dim(x, member + 1 - 2 * index["core"], 0, keepdims=False)
    far = lax.dynamic_slice_in_dim(x, 2 - index["xl"] * 2, 2, 0)

    row = lax.dynamic_index_in_dim(modulation[0, 0], timestep[0], 0, keepdims=False)
    mod = row[: 2 * D].reshape(2, D)
    gate = lax.dynamic_slice_in_dim(row, 2 * D + member * PART, PART, 0).reshape(1, PART)

    lane = jnp.arange(GROUP, dtype=jnp.int32)
    source = lane // LOCAL
    patch = (source // 2 * 4 + index["yh"]) * 2 + source % 2
    blocks = patch * (LOCAL // ROWS) + lane % LOCAL // ROWS
    positions = (patch_order[index["xh"] * (TOKENS // 2 // ROWS) + blocks] * ROWS + lane % ROWS).astype(jnp.float32)
    halfway = HDIM // 2
    inverse = jnp.exp(-math.log(10000.0) * jnp.arange(halfway, dtype=jnp.float32) / halfway)
    angles = positions[:, None] * inverse[None, :]
    cosine, sine = jnp.cos(angles), jnp.sin(angles)
    cosine = jnp.concatenate([cosine, cosine], axis=1)
    sine = jnp.concatenate([-sine, sine], axis=1)

    fresh = jnp.zeros((GROUP, 2 * PART), jnp.bfloat16)
    for tick in range(SECTIONS):
        state, fresh = run_block(tick, who, near, cross, far, weight, kv, kv_other, mod, gate, cosine, sine, blocks[:, None], fresh)
        if tick == 0:
            moved, state = lax.optimization_barrier((early[1] + late[1], state))
            weight = place(early[0] + late[0], "rest", where, moved, [weight])
        if tick + 1 < SECTIONS:
            far = lax.ppermute(state, AXES, onward(tick, 1, 0))
            near = lax.ppermute(state, AXES, onward(tick, 0, 0))
            cross = lax.ppermute(state, AXES, onward(tick, 0, 1))
            far = lax.all_gather(far, "core", axis=0, tiled=False)

    ends = lax.all_gather(state, ("xl", "core"), axis=0, tiled=False)
    finals = lax.dynamic_slice_in_dim(ends, member * LOCAL, LOCAL, 1)
    finals = jnp.transpose(finals, (1, 0, 2)).reshape(SECTIONS, LOCAL // SECTIONS, 2, D // 2)
    finals = jnp.transpose(finals, (0, 2, 1, 3)).reshape(SECTIONS * 2, LOCAL // SECTIONS, D // 2)
    spread = lax.all_to_all(finals, ("section", "cfg"), split_axis=0, concat_axis=0, tiled=True)
    kept = lax.all_gather(fresh, ("xl", "core"), axis=0, tiled=False)
    kept = lax.dynamic_slice_in_dim(kept, member * LOCAL, LOCAL, 1)
    kept = jnp.transpose(kept.reshape(MEMBERS, LOCAL, 2, PART), (1, 2, 0, 3)).reshape(LOCAL, 2 * D)
    spread, kept = lax.optimization_barrier((spread, kept))
    uncond = spread[2 * SECTIONS - 2].astype(jnp.float32)
    conditioned = spread[2 * SECTIONS - 1].astype(jnp.float32)
    guided = (uncond + guide_weight * (conditioned - uncond)).astype(jnp.bfloat16)
    return guided, kept[None, None]


def solution(mesh):
    fine = Mesh(mesh.devices.reshape(SIZES), AXES)
    patch = ("xh", "xl", "yh", "core")
    return jax.shard_map(
        body,
        mesh=fine,
        in_specs=(
            P("cfg", patch, None),
            P(),
            P(),
            P("section", "cfg", None, None),
            P("section", None, patch),
            P("section", "cfg", patch, None),
        ),
        out_specs=(P((*patch, "section"), "cfg"), P("section", "cfg", patch, None)),
        check_vma=False,
    )
```

```python
import functools
import math

import jax
import jax.numpy as jnp
import numpy as np
from jax import lax
from jax.experimental import pallas as pl
from jax.experimental.pallas import tpu as pltpu
from jax.sharding import Mesh, PartitionSpec as P

HEADS = 12
HDIM = 128
ROWS = 8
D = HEADS * HDIM
TOKENS = 512
SECTIONS = 8
MEMBERS = 4
PART = D // MEMBERS
LOCAL = 16
GROUP = LOCAL * MEMBERS
UNIT = 48
UNITS = 3
COLUMNS = UNIT * UNITS
HALF = D // 2
BLOCK = 2 * COLUMNS

guide_weight = 3.5
norm_eps = 1e-06

AXES = ("xh", "xl", "yh", "core", "section", "cfg")
SIZES = (2, 2, 4, 2, 8, 2)


def route(step):
    def number(x, y, core, section):
        return (((x * 4 + y // 2) * 2 + core) * 8 + section) * 2 + y % 2

    return [
        (number(x, y, core, s), number(*step(x, y, core), s))
        for x in range(4)
        for y in range(8)
        for core in range(2)
        for s in range(SECTIONS)
    ]


def member_at(x, y, core, row):
    return (((y // 2 * 2 + core) * COLUMNS + row) // PART - x) % 4


def spread(copy, row):
    def step(x, y, core):
        member = member_at(x, y, core, row(y, core))
        return (copy(core) * 2 + member // 2, y, member % 2)

    return route(step)


def cut(y, core):
    if (y // 2, core) == (1, 0):
        return 1, 2 * UNIT, 0
    if (y // 2, core) == (2, 1):
        return 1, 0, UNIT
    return 0, 0, 0


MAIN = [spread(lambda core, k=k: core ^ k, lambda y, core: cut(y, core)[2]) for k in range(2)]
TURN = [spread(lambda core, k=k: k, lambda y, core: cut(y, core)[1]) for k in range(2)]
_CUTS = {n for n in range(512) if cut(n // 16 // 2 % 4 * 2 + n % 2, n // 16 % 2)[0]}
TURN = [[edge for edge in edges if edge[0] in _CUTS] for edges in TURN]
UP = route(lambda x, y, core: (x, (y + 1 - 2 * core) % 8, core))
DOWN = route(lambda x, y, core: (x, (y - 1 + 2 * core) % 8, core))
ACROSS = [(i, (i + 256) % 512) for i in range(512)]


def place_of(x, y, core, section):
    return (((x * 4 + y // 2) * 2 + core) * 8 + section) * 2 + y % 2


PLANE = [(x, y, core) for x in range(4) for y in range(8) for core in range(2)]
LAST = SECTIONS - 1


def onward(tick, flip, turn):
    return [
        (place_of(x, y, core, section), place_of(x ^ flip, y, core ^ turn, section + 1))
        for section in range(tick % 4, LAST, 4)
        for x, y, core in PLANE
    ]


def nt_dot(a, b):
    return lax.dot_general(a, b, (((1,), (1,)), ((), ())), preferred_element_type=jnp.float32)


def block_kernel(tick, who, near_ref, cross_ref, far_ref, w_ref, kv_ref, other_ref, mod_ref, gate_ref, cos_ref, sin_ref, block_ref, old_ref, state_ref, fresh_ref):
    active = who[1] == tick

    @pl.when(jnp.logical_not(active))
    def _():
        fresh_ref[...] = old_ref[...]

    @pl.when(active)
    def _():
        active_block(who[0], near_ref, cross_ref, far_ref, w_ref, kv_ref, other_ref, mod_ref, gate_ref, cos_ref, sin_ref, block_ref, state_ref, fresh_ref)


def active_block(member, near_ref, cross_ref, far_ref, w_ref, kv_ref, other_ref, mod_ref, gate_ref, cos_ref, sin_ref, block_ref, state_ref, fresh_ref):
    near, cross = near_ref[...].astype(jnp.float32), cross_ref[...].astype(jnp.float32)
    first = member % 2 == 0
    near = [jnp.where(first, near, cross), jnp.where(first, cross, near)]
    far = [far_ref[core].astype(jnp.float32) for core in range(2)]
    low = member < 2
    xs = [jnp.where(low, near[core], far[core]) for core in range(2)]
    xs += [jnp.where(low, far[core], near[core]) for core in range(2)]
    center = sum(jnp.sum(x, axis=-1, keepdims=True) for x in xs) / D
    xs = [x - center for x in xs]
    spread = sum(jnp.sum(x * x, axis=-1, keepdims=True) for x in xs) / D
    inv = lax.rsqrt(spread + norm_eps)
    normed = jnp.concatenate(
        [
            (
                xs[i] * inv * (1.0 + mod_ref[1:2, i * PART : (i + 1) * PART])
                + mod_ref[0:1, i * PART : (i + 1) * PART]
            ).astype(jnp.bfloat16)
            for i in range(MEMBERS)
        ],
        axis=1,
    )
    projected = jnp.dot(normed, w_ref[...], preferred_element_type=jnp.float32).astype(jnp.bfloat16)
    row_block = block_ref[...]
    stale_mask = lax.broadcasted_iota(jnp.int32, (GROUP, TOKENS // 2), 1) // ROWS == row_block
    own_mask = (
        lax.broadcasted_iota(jnp.int32, (GROUP, GROUP), 0) // ROWS
        == lax.broadcasted_iota(jnp.int32, (GROUP, GROUP), 1) // ROWS
    )
    cosine, sine = cos_ref[...], sin_ref[...]

    def turned(values):
        values = values.astype(jnp.float32)
        values = values * lax.rsqrt(jnp.mean(values * values, axis=-1, keepdims=True) + norm_eps)
        return (values * cosine + pltpu.roll(values, HDIM // 2, 1) * sine).astype(jnp.bfloat16)

    heads = range(PART // HDIM)
    cols = [slice(h * HDIM, (h + 1) * HDIM) for h in heads]
    vcols = [slice(PART + h * HDIM, PART + (h + 1) * HDIM) for h in heads]
    scale = 1.0 / math.sqrt(HDIM)
    query = [turned(projected[:, cols[h]]) for h in heads]
    key = [turned(projected[:, vcols[h]]) for h in heads]
    value = [projected[:, 2 * PART + h * HDIM : 2 * PART + (h + 1) * HDIM] for h in heads]
    scores = [nt_dot(query[h], kv_ref[:, cols[h]]) for h in heads]
    other_scores = [nt_dot(query[h], other_ref[:, cols[h]]) for h in heads]
    own_scores = [nt_dot(query[h], key[h]) for h in heads]
    weights = [jnp.where(stale_mask, 0.0, jnp.exp(scores[h] * scale)) for h in heads]
    others = [jnp.exp(other_scores[h] * scale) for h in heads]
    own = [jnp.where(own_mask, jnp.exp(own_scores[h] * scale), 0.0) for h in heads]
    total = [
        jnp.sum(weights[h] + others[h], axis=-1, keepdims=True) + jnp.sum(own[h], axis=-1, keepdims=True)
        for h in heads
    ]
    attended = [
        jnp.dot(weights[h].astype(jnp.bfloat16), kv_ref[:, vcols[h]], preferred_element_type=jnp.float32)
        + jnp.dot(others[h].astype(jnp.bfloat16), other_ref[:, vcols[h]], preferred_element_type=jnp.float32)
        + jnp.dot(own[h].astype(jnp.bfloat16), value[h], preferred_element_type=jnp.float32)
        for h in heads
    ]
    for h in heads:
        state = near_ref[:, cols[h]].astype(jnp.float32) + gate_ref[0:1, cols[h]] * (attended[h] / total[h])
        state_ref[:, cols[h]] = state.astype(jnp.bfloat16)
        fresh_ref[:, cols[h]] = key[h]
        fresh_ref[:, vcols[h]] = value[h]


def run_block(tick, who, near, cross, far, weight, kv, other, mod, gate, cosine, sine, blocks, old):
    vmem = pl.BlockSpec(memory_space=pltpu.VMEM)
    weight = pltpu.with_memory_space_constraint(weight, pltpu.VMEM)
    return pl.pallas_call(
        functools.partial(block_kernel, tick),
        out_shape=(
            jax.ShapeDtypeStruct((GROUP, PART), jnp.bfloat16),
            jax.ShapeDtypeStruct((GROUP, 2 * PART), jnp.bfloat16),
        ),
        in_specs=[pl.BlockSpec(memory_space=pltpu.SMEM)] + [vmem] * 12,
        out_specs=(vmem, vmem),
        compiler_params=pltpu.CompilerParams(vmem_limit_bytes=8 * 1024 * 1024),
        name="block_step",
    )(who, near, cross, far, weight, kv, other, mod, gate, cosine, sine, blocks, old)


def half_kernel(where, columns_ref, half_ref, turn_ref, sems):
    first = jnp.where(where[2] == 0, 2 * UNIT, 0)
    col = pl.ds(pl.multiple_of(where[3] % 2 * HALF, 128), HALF)
    whole = pltpu.make_async_copy(columns_ref.at[:, col], half_ref, sems.at[0])
    turn = pltpu.make_async_copy(
        columns_ref.at[pl.ds(pl.multiple_of(first, 16), UNIT), col], turn_ref, sems.at[1]
    )
    whole.start()
    turn.start()
    whole.wait()
    turn.wait()


def stale_kernel(where, stale_ref, out_ref, sem):
    copies = []
    for slot in range(2 * 4 * 2):
        m = slot // 8 * 2 + slot % 2
        for part in range(2):
            copies.append(
                pltpu.make_async_copy(
                    stale_ref.at[:, part * D + m * PART : part * D + (m + 1) * PART],
                    out_ref.at[slot, :, part * PART : (part + 1) * PART],
                    sem,
                )
            )
            copies[-1].start()
    for copy in copies:
        copy.wait()


def join_kernel(where, first_ref, second_ref, turn0_ref, turn1_ref, own_ref):
    half, y = where[1], where[3]

    def pick(one, two):
        return jnp.where(half == 0, one[...], two[...])

    own_ref[:COLUMNS, :] = pick(first_ref, second_ref)
    own_ref[COLUMNS:, :] = pick(second_ref, first_ref)

    @pl.when(y // 2 == 1)
    def _():
        own_ref[2 * UNIT : COLUMNS, :] = pick(turn0_ref, turn1_ref)

    @pl.when(y // 2 == 2)
    def _():
        own_ref[COLUMNS : COLUMNS + UNIT, :] = pick(turn0_ref, turn1_ref)


def place_kernel(sources, kind, where, *refs):
    blocks, refs = refs[: len(sources)], refs[len(sources) :]
    rows = refs[{"first": 0, "last": 1, "rest": 2}[kind]]
    sem = refs[-1]
    member, core, y, later = where[0], where[2], where[3], where[4]
    sign = 1 - 2 * core

    def home(unit):
        third = unit // 8
        part = (COLUMNS * 8 * ((third - member + 4) % 4) + PART * third) // D
        return part * PART + unit % 8 * UNIT

    @pl.when(later == (1 if kind == "rest" else 0))
    def _():
        copies = []
        for (source, parts), ref in zip(sources, blocks):
            at = (y + sign * source + 8) % 8
            col = pl.ds(pl.multiple_of(at % 2 * HALF, 128), HALF)
            for n, part in enumerate(parts):
                for j in range(UNITS):
                    row = pl.multiple_of(home((at // 2 * 2 + part) * UNITS + j), 16)
                    copy = pltpu.make_async_copy(
                        ref.at[pl.ds(n * COLUMNS + j * UNIT, UNIT)], rows.at[pl.ds(row, UNIT), col], sem
                    )
                    copy.start()
                    copies.append(copy)
        for copy in copies:
            copy.wait()
        if kind != "first":
            out_ref = refs[2 if kind == "last" else 1]
            for c in range(0, D, HDIM):
                out_ref[c : c + HDIM, :] = jnp.transpose(rows[:, c : c + HDIM])


def place(sources, kind, where, blocks, held=()):
    any_space = pl.BlockSpec(memory_space=pl.ANY)
    vmem = pl.BlockSpec(memory_space=pltpu.VMEM)
    whole = jax.ShapeDtypeStruct((3 * PART, D), jnp.bfloat16)
    turned = jax.ShapeDtypeStruct((D, 3 * PART), jnp.bfloat16)
    scratch = [pltpu.SemaphoreType.DMA]
    if kind == "rest":
        scratch = [pltpu.VMEM((3 * PART, D), jnp.bfloat16), *scratch]
    return pl.pallas_call(
        functools.partial(place_kernel, sources, kind),
        out_shape={"first": whole, "last": (whole, turned), "rest": turned}[kind],
        in_specs=[pl.BlockSpec(memory_space=pltpu.SMEM)] + [any_space] * len(blocks) + [vmem] * len(held),
        out_specs=(vmem, vmem) if kind == "last" else vmem,
        input_output_aliases={len(blocks) + 1: 0} if held else {},
        scratch_shapes=scratch,
        compiler_params=pltpu.CompilerParams(vmem_limit_bytes=12 * 1024 * 1024),
        name="place_" + kind,
    )(where, *blocks, *held)


def renew_kernel(weight_ref, out_ref, sem):
    copy = pltpu.make_async_copy(weight_ref, out_ref, sem)
    copy.start()
    copy.wait()


def renew(weight):
    vmem = pl.BlockSpec(memory_space=pltpu.VMEM)
    return pl.pallas_call(
        renew_kernel,
        out_shape=jax.ShapeDtypeStruct(weight.shape, weight.dtype),
        in_specs=[vmem],
        out_specs=vmem,
        scratch_shapes=[pltpu.SemaphoreType.DMA],
        compiler_params=pltpu.CompilerParams(vmem_limit_bytes=8 * 1024 * 1024),
        name="renew_weight",
    )(pltpu.with_memory_space_constraint(weight, pltpu.VMEM))


def whole_call(kernel, where, arrays, outs, sems=()):
    vmem = pl.BlockSpec(memory_space=pltpu.VMEM)
    held = pl.BlockSpec(memory_space=pl.ANY) if sems else vmem
    return pl.pallas_call(
        kernel,
        out_shape=[jax.ShapeDtypeStruct(shape, jnp.bfloat16) for shape in outs],
        in_specs=[pl.BlockSpec(memory_space=pltpu.SMEM)] + [held] * len(arrays),
        out_specs=[vmem] * len(outs),
        scratch_shapes=list(sems),
        compiler_params=pltpu.CompilerParams(vmem_limit_bytes=8 * 1024 * 1024),
        name=kernel.__name__,
    )(where, *arrays)


def body(hidden, timestep, patch_order, modulation, qkv_weight, stale_kv):
    index = {a: lax.axis_index(a) for a in AXES}
    section = index["section"]
    member = index["xl"] * 2 + index["core"]
    y = index["yh"] * 2 + index["cfg"]
    where = jnp.stack([member, index["xh"], index["core"], y, jnp.minimum(section, 1)]).astype(jnp.int32)
    who = jnp.stack([member, section]).astype(jnp.int32)

    half, turn = whole_call(
        half_kernel,
        where,
        [jnp.transpose(qkv_weight[0])],
        [(COLUMNS, HALF), (UNIT, HALF)],
        [pltpu.SemaphoreType.DMA((2,))],
    )
    moved = [lax.ppermute(half, AXES, edges) for edges in MAIN]
    turned = [lax.ppermute(turn, AXES, edges) for edges in TURN]
    (outgoing,) = whole_call(
        stale_kernel, where, [stale_kv[0, 0]], [(2 * 4 * 2, LOCAL, 2 * PART)], [pltpu.SemaphoreType.DMA]
    )
    kv = lax.all_to_all(outgoing, ("xl", "yh", "core"), split_axis=0, concat_axis=0, tiled=True)
    kv = kv.reshape(TOKENS // 2, 2 * PART)
    (own,) = whole_call(join_kernel, where, [*moved, *turned], [(BLOCK, HALF)])
    up1, down1 = lax.ppermute(own, AXES, UP), lax.ppermute(own, AXES, DOWN)
    up1, entering, kv = lax.optimization_barrier((up1, hidden[0], kv))
    kv_other = lax.ppermute(kv, AXES, ACROSS)
    x = lax.all_gather(entering, ("xl", "core"), axis=0, tiled=True)
    up2, down2 = lax.ppermute(up1, AXES, UP), lax.ppermute(down1, AXES, DOWN)
    down2, x = lax.optimization_barrier((down2, x))
    up3, down3 = lax.ppermute(up2, AXES, UP), lax.ppermute(down2, AXES, DOWN)
    up4 = lax.ppermute(up3[:COLUMNS], AXES, UP)
    down4 = lax.ppermute(down3[COLUMNS:], AXES, DOWN)
    both = (0, 1)
    early = ((0, both), (-1, both), (1, both), (-2, both), (2, both)), [own, up1, down1, up2, down2]
    late = ((-3, both), (3, both), (4, (0,)), (4, (1,))), [up3, down3, up4, down4]
    rows = place(early[0], "first", where, early[1])
    _, weight = place(late[0], "last", where, late[1], [rows])
    x = jnp.transpose(x.reshape(GROUP, MEMBERS, PART), (1, 0, 2))
    near = lax.dynamic_index_in_dim(x, member, 0, keepdims=False)
    cross = lax.dynamic_index_in_dim(x, member + 1 - 2 * index["core"], 0, keepdims=False)
    far = lax.dynamic_slice_in_dim(x, 2 - index["xl"] * 2, 2, 0)

    row = lax.dynamic_index_in_dim(modulation[0, 0], timestep[0], 0, keepdims=False)
    mod = row[: 2 * D].reshape(2, D)
    gate = lax.dynamic_slice_in_dim(row, 2 * D + member * PART, PART, 0).reshape(1, PART)

    lane = jnp.arange(GROUP, dtype=jnp.int32)
    source = lane // LOCAL
    patch = (source // 2 * 4 + index["yh"]) * 2 + source % 2
    blocks = patch * (LOCAL // ROWS) + lane % LOCAL // ROWS
    positions = (patch_order[index["xh"] * (TOKENS // 2 // ROWS) + blocks] * ROWS + lane % ROWS).astype(jnp.float32)
    halfway = HDIM // 2
    inverse = jnp.exp(-math.log(10000.0) * jnp.arange(halfway, dtype=jnp.float32) / halfway)
    angles = positions[:, None] * inverse[None, :]
    cosine, sine = jnp.cos(angles), jnp.sin(angles)
    cosine = jnp.concatenate([cosine, cosine], axis=1)
    sine = jnp.concatenate([-sine, sine], axis=1)

    fresh = jnp.zeros((GROUP, 2 * PART), jnp.bfloat16)
    for tick in range(SECTIONS):
        state, fresh = run_block(tick, who, near, cross, far, weight, kv, kv_other, mod, gate, cosine, sine, blocks[:, None], fresh)
        if tick == 0:
            moved, state = lax.optimization_barrier((early[1] + late[1], state))
            weight = place(early[0] + late[0], "rest", where, moved, [weight])
        if tick == SECTIONS - 2:
            state, weight = lax.optimization_barrier((state, weight))
            weight = renew(weight)
        if tick + 1 < SECTIONS:
            far = lax.ppermute(state, AXES, onward(tick, 1, 0))
            near = lax.ppermute(state, AXES, onward(tick, 0, 0))
            cross = lax.ppermute(state, AXES, onward(tick, 0, 1))
            far = lax.all_gather(far, "core", axis=0, tiled=False)

    ends = lax.all_gather(state, ("xl", "core"), axis=0, tiled=False)
    finals = lax.dynamic_slice_in_dim(ends, member * LOCAL, LOCAL, 1)
    finals = jnp.transpose(finals, (1, 0, 2)).reshape(SECTIONS, LOCAL // SECTIONS, 2, D // 2)
    finals = jnp.transpose(finals, (0, 2, 1, 3)).reshape(SECTIONS * 2, LOCAL // SECTIONS, D // 2)
    spread = lax.all_to_all(finals, ("section", "cfg"), split_axis=0, concat_axis=0, tiled=True)
    kept = lax.all_gather(fresh, ("xl", "core"), axis=0, tiled=False)
    kept = lax.dynamic_slice_in_dim(kept, member * LOCAL, LOCAL, 1)
    kept = jnp.transpose(kept.reshape(MEMBERS, LOCAL, 2, PART), (1, 2, 0, 3)).reshape(LOCAL, 2 * D)
    spread, kept = lax.optimization_barrier((spread, kept))
    uncond = spread[2 * SECTIONS - 2].astype(jnp.float32)
    conditioned = spread[2 * SECTIONS - 1].astype(jnp.float32)
    guided = (uncond + guide_weight * (conditioned - uncond)).astype(jnp.bfloat16)
    return guided, kept[None, None]


def solution(mesh):
    fine = Mesh(mesh.devices.reshape(SIZES), AXES)
    patch = ("xh", "xl", "yh", "core")
    return jax.shard_map(
        body,
        mesh=fine,
        in_specs=(
            P("cfg", patch, None),
            P(),
            P(),
            P("section", "cfg", None, None),
            P("section", None, patch),
            P("section", "cfg", patch, None),
        ),
        out_specs=(P((*patch, "section"), "cfg"), P("section", "cfg", patch, None)),
        check_vma=False,
    )
```

```python
import functools
import math

import jax
import jax.numpy as jnp
import numpy as np
from jax import lax
from jax.experimental import pallas as pl
from jax.experimental.pallas import tpu as pltpu
from jax.sharding import Mesh, PartitionSpec as P

HEADS = 12
HDIM = 128
ROWS = 8
D = HEADS * HDIM
TOKENS = 512
SECTIONS = 8
MEMBERS = 4
PART = D // MEMBERS
LOCAL = 16
GROUP = LOCAL * MEMBERS
UNIT = 48
UNITS = 3
COLUMNS = UNIT * UNITS
HALF = D // 2
BLOCK = 2 * COLUMNS

guide_weight = 3.5
norm_eps = 1e-06

AXES = ("xh", "xl", "yh", "core", "section", "cfg")
SIZES = (2, 2, 4, 2, 8, 2)


def route(step):
    def number(x, y, core, section):
        return (((x * 4 + y // 2) * 2 + core) * 8 + section) * 2 + y % 2

    return [
        (number(x, y, core, s), number(*step(x, y, core), s))
        for x in range(4)
        for y in range(8)
        for core in range(2)
        for s in range(SECTIONS)
    ]


def member_at(x, y, core, row):
    return (((y // 2 * 2 + core) * COLUMNS + row) // PART - x) % 4


def spread(copy, row):
    def step(x, y, core):
        member = member_at(x, y, core, row(y, core))
        return (copy(core) * 2 + member // 2, y, member % 2)

    return route(step)


def cut(y, core):
    if (y // 2, core) == (1, 0):
        return 1, 2 * UNIT, 0
    if (y // 2, core) == (2, 1):
        return 1, 0, UNIT
    return 0, 0, 0


MAIN = [spread(lambda core, k=k: core ^ k, lambda y, core: cut(y, core)[2]) for k in range(2)]
TURN = [spread(lambda core, k=k: k, lambda y, core: cut(y, core)[1]) for k in range(2)]
_CUTS = {n for n in range(512) if cut(n // 16 // 2 % 4 * 2 + n % 2, n // 16 % 2)[0]}
TURN = [[edge for edge in edges if edge[0] in _CUTS] for edges in TURN]
UP = route(lambda x, y, core: (x, (y + 1 - 2 * core) % 8, core))
DOWN = route(lambda x, y, core: (x, (y - 1 + 2 * core) % 8, core))
ACROSS = [(i, (i + 256) % 512) for i in range(512)]


def place_of(x, y, core, section):
    return (((x * 4 + y // 2) * 2 + core) * 8 + section) * 2 + y % 2


PLANE = [(x, y, core) for x in range(4) for y in range(8) for core in range(2)]
LAST = SECTIONS - 1


def onward(tick, flip, turn):
    return [
        (place_of(x, y, core, section), place_of(x ^ flip, y, core ^ turn, section + 1))
        for section in range(tick % 4, LAST, 4)
        for x, y, core in PLANE
    ]


def nt_dot(a, b):
    return lax.dot_general(a, b, (((1,), (1,)), ((), ())), preferred_element_type=jnp.float32)


def block_kernel(tick, near_ref, cross_ref, far_ref, w_ref, kv_ref, other_ref, mod_ref, gate_ref, cos_ref, sin_ref, block_ref, old_ref, state_ref, fresh_ref):
    active = lax.axis_index("section") == tick
    member = lax.axis_index("xl") * 2 + lax.axis_index("core")

    @pl.when(jnp.logical_not(active))
    def _():
        fresh_ref[...] = old_ref[...]

    @pl.when(active)
    def _():
        active_block(member, near_ref, cross_ref, far_ref, w_ref, kv_ref, other_ref, mod_ref, gate_ref, cos_ref, sin_ref, block_ref, state_ref, fresh_ref)


def active_block(member, near_ref, cross_ref, far_ref, w_ref, kv_ref, other_ref, mod_ref, gate_ref, cos_ref, sin_ref, block_ref, state_ref, fresh_ref):
    near, cross = near_ref[...].astype(jnp.float32), cross_ref[...].astype(jnp.float32)
    first = member % 2 == 0
    near = [jnp.where(first, near, cross), jnp.where(first, cross, near)]
    far = [far_ref[core].astype(jnp.float32) for core in range(2)]
    low = member < 2
    xs = [jnp.where(low, near[core], far[core]) for core in range(2)]
    xs += [jnp.where(low, far[core], near[core]) for core in range(2)]
    center = sum(jnp.sum(x, axis=-1, keepdims=True) for x in xs) / D
    xs = [x - center for x in xs]
    spread = sum(jnp.sum(x * x, axis=-1, keepdims=True) for x in xs) / D
    inv = lax.rsqrt(spread + norm_eps)
    normed = jnp.concatenate(
        [
            (
                xs[i] * inv * (1.0 + mod_ref[1:2, i * PART : (i + 1) * PART])
                + mod_ref[0:1, i * PART : (i + 1) * PART]
            ).astype(jnp.bfloat16)
            for i in range(MEMBERS)
        ],
        axis=1,
    )
    projected = jnp.dot(normed, w_ref[...], preferred_element_type=jnp.float32).astype(jnp.bfloat16)
    row_block = block_ref[...]
    stale_mask = lax.broadcasted_iota(jnp.int32, (GROUP, TOKENS // 2), 1) // ROWS == row_block
    own_mask = (
        lax.broadcasted_iota(jnp.int32, (GROUP, GROUP), 0) // ROWS
        == lax.broadcasted_iota(jnp.int32, (GROUP, GROUP), 1) // ROWS
    )
    cosine, sine = cos_ref[...], sin_ref[...]

    def turned(values):
        values = values.astype(jnp.float32)
        values = values * lax.rsqrt(jnp.mean(values * values, axis=-1, keepdims=True) + norm_eps)
        return (values * cosine + pltpu.roll(values, HDIM // 2, 1) * sine).astype(jnp.bfloat16)

    heads = range(PART // HDIM)
    cols = [slice(h * HDIM, (h + 1) * HDIM) for h in heads]
    vcols = [slice(PART + h * HDIM, PART + (h + 1) * HDIM) for h in heads]
    scale = 1.0 / math.sqrt(HDIM)
    query = [turned(projected[:, cols[h]]) for h in heads]
    key = [turned(projected[:, vcols[h]]) for h in heads]
    value = [projected[:, 2 * PART + h * HDIM : 2 * PART + (h + 1) * HDIM] for h in heads]
    scores = [nt_dot(query[h], kv_ref[:, cols[h]]) for h in heads]
    other_scores = [nt_dot(query[h], other_ref[:, cols[h]]) for h in heads]
    own_scores = [nt_dot(query[h], key[h]) for h in heads]
    weights = [jnp.where(stale_mask, 0.0, jnp.exp(scores[h] * scale)) for h in heads]
    others = [jnp.exp(other_scores[h] * scale) for h in heads]
    own = [jnp.where(own_mask, jnp.exp(own_scores[h] * scale), 0.0) for h in heads]
    total = [
        jnp.sum(weights[h] + others[h], axis=-1, keepdims=True) + jnp.sum(own[h], axis=-1, keepdims=True)
        for h in heads
    ]
    attended = [
        jnp.dot(weights[h].astype(jnp.bfloat16), kv_ref[:, vcols[h]], preferred_element_type=jnp.float32)
        + jnp.dot(others[h].astype(jnp.bfloat16), other_ref[:, vcols[h]], preferred_element_type=jnp.float32)
        + jnp.dot(own[h].astype(jnp.bfloat16), value[h], preferred_element_type=jnp.float32)
        for h in heads
    ]
    for h in heads:
        state = near_ref[:, cols[h]].astype(jnp.float32) + gate_ref[0:1, cols[h]] * (attended[h] / total[h])
        state_ref[:, cols[h]] = state.astype(jnp.bfloat16)
        fresh_ref[:, cols[h]] = key[h]
        fresh_ref[:, vcols[h]] = value[h]


def run_block(tick, near, cross, far, weight, kv, other, mod, gate, cosine, sine, blocks, old):
    vmem = pl.BlockSpec(memory_space=pltpu.VMEM)
    weight = pltpu.with_memory_space_constraint(weight, pltpu.VMEM)
    return pl.pallas_call(
        functools.partial(block_kernel, tick),
        out_shape=(
            jax.ShapeDtypeStruct((GROUP, PART), jnp.bfloat16),
            jax.ShapeDtypeStruct((GROUP, 2 * PART), jnp.bfloat16),
        ),
        in_specs=[vmem] * 12,
        out_specs=(vmem, vmem),
        compiler_params=pltpu.CompilerParams(vmem_limit_bytes=8 * 1024 * 1024),
        name="block_step",
    )(near, cross, far, weight, kv, other, mod, gate, cosine, sine, blocks, old)


def seat():
    y = lax.axis_index("yh") * 2 + lax.axis_index("cfg")
    core = lax.axis_index("core")
    later = jnp.minimum(lax.axis_index("section"), 1)
    return lax.axis_index("xl") * 2 + core, lax.axis_index("xh"), core, y, later


def half_kernel(columns_ref, half_ref, turn_ref, sems):
    _, _, core, y, _ = seat()
    first = (1 - core) * (2 * UNIT)
    col = pl.ds(pl.multiple_of(y % 2 * HALF, 128), HALF)
    whole = pltpu.make_async_copy(columns_ref.at[:, col], half_ref, sems.at[0])
    turn = pltpu.make_async_copy(
        columns_ref.at[pl.ds(pl.multiple_of(first, 16), UNIT), col], turn_ref, sems.at[1]
    )
    whole.start()
    turn.start()
    whole.wait()
    turn.wait()


def stale_kernel(stale_ref, out_ref, sem):
    copies = []
    for slot in range(2 * 4 * 2):
        m = slot // 8 * 2 + slot % 2
        for part in range(2):
            copies.append(
                pltpu.make_async_copy(
                    stale_ref.at[:, part * D + m * PART : part * D + (m + 1) * PART],
                    out_ref.at[slot, :, part * PART : (part + 1) * PART],
                    sem,
                )
            )
            copies[-1].start()
    for copy in copies:
        copy.wait()


def join_kernel(first_ref, second_ref, turn0_ref, turn1_ref, own_ref):
    _, half, _, y, _ = seat()

    def pick(one, two):
        return jnp.where(half == 0, one[...], two[...])

    own_ref[:COLUMNS, :] = pick(first_ref, second_ref)
    own_ref[COLUMNS:, :] = pick(second_ref, first_ref)

    @pl.when(y // 2 == 1)
    def _():
        own_ref[2 * UNIT : COLUMNS, :] = pick(turn0_ref, turn1_ref)

    @pl.when(y // 2 == 2)
    def _():
        own_ref[COLUMNS : COLUMNS + UNIT, :] = pick(turn0_ref, turn1_ref)


def place_kernel(sources, kind, *refs):
    blocks, refs = refs[: len(sources)], refs[len(sources) :]
    rows = refs[{"first": 0, "last": 1, "rest": 2}[kind]]
    sem = refs[-1]
    member, _, core, y, later = seat()
    sign = 1 - 2 * core

    def home(unit):
        third = unit // 8
        part = (COLUMNS * 8 * ((third - member + 4) % 4) + PART * third) // D
        return part * PART + unit % 8 * UNIT

    @pl.when(later == (1 if kind == "rest" else 0))
    def _():
        copies = []
        for (source, parts), ref in zip(sources, blocks):
            at = (y + sign * source + 8) % 8
            col = pl.ds(pl.multiple_of(at % 2 * HALF, 128), HALF)
            for n, part in enumerate(parts):
                for j in range(UNITS):
                    row = pl.multiple_of(home((at // 2 * 2 + part) * UNITS + j), 16)
                    copy = pltpu.make_async_copy(
                        ref.at[pl.ds(n * COLUMNS + j * UNIT, UNIT)], rows.at[pl.ds(row, UNIT), col], sem
                    )
                    copy.start()
                    copies.append(copy)
        for copy in copies:
            copy.wait()
        if kind != "first":
            out_ref = refs[2 if kind == "last" else 1]
            for c in range(0, D, HDIM):
                out_ref[c : c + HDIM, :] = jnp.transpose(rows[:, c : c + HDIM])


def place(sources, kind, blocks, held=()):
    any_space = pl.BlockSpec(memory_space=pl.ANY)
    vmem = pl.BlockSpec(memory_space=pltpu.VMEM)
    whole = jax.ShapeDtypeStruct((3 * PART, D), jnp.bfloat16)
    turned = jax.ShapeDtypeStruct((D, 3 * PART), jnp.bfloat16)
    scratch = [pltpu.SemaphoreType.DMA]
    if kind == "rest":
        scratch = [pltpu.VMEM((3 * PART, D), jnp.bfloat16), *scratch]
    return pl.pallas_call(
        functools.partial(place_kernel, sources, kind),
        out_shape={"first": whole, "last": (whole, turned), "rest": turned}[kind],
        in_specs=[any_space] * len(blocks) + [vmem] * len(held),
        out_specs=(vmem, vmem) if kind == "last" else vmem,
        input_output_aliases={len(blocks): 0} if held else {},
        scratch_shapes=scratch,
        compiler_params=pltpu.CompilerParams(vmem_limit_bytes=12 * 1024 * 1024),
        name="place_" + kind,
    )(*blocks, *held)


def renew_kernel(weight_ref, out_ref, sem):
    copy = pltpu.make_async_copy(weight_ref, out_ref, sem)
    copy.start()
    copy.wait()


def renew(weight):
    vmem = pl.BlockSpec(memory_space=pltpu.VMEM)
    return pl.pallas_call(
        renew_kernel,
        out_shape=jax.ShapeDtypeStruct(weight.shape, weight.dtype),
        in_specs=[vmem],
        out_specs=vmem,
        scratch_shapes=[pltpu.SemaphoreType.DMA],
        compiler_params=pltpu.CompilerParams(vmem_limit_bytes=8 * 1024 * 1024),
        name="renew_weight",
    )(pltpu.with_memory_space_constraint(weight, pltpu.VMEM))


def whole_call(kernel, arrays, outs, sems=()):
    vmem = pl.BlockSpec(memory_space=pltpu.VMEM)
    held = pl.BlockSpec(memory_space=pl.ANY) if sems else vmem
    return pl.pallas_call(
        kernel,
        out_shape=[jax.ShapeDtypeStruct(shape, jnp.bfloat16) for shape in outs],
        in_specs=[held] * len(arrays),
        out_specs=[vmem] * len(outs),
        scratch_shapes=list(sems),
        compiler_params=pltpu.CompilerParams(vmem_limit_bytes=8 * 1024 * 1024),
        name=kernel.__name__,
    )(*arrays)


def body(hidden, timestep, patch_order, modulation, qkv_weight, stale_kv):
    index = {a: lax.axis_index(a) for a in AXES}
    section = index["section"]
    member = index["xl"] * 2 + index["core"]

    half, turn = whole_call(
        half_kernel,
        [jnp.transpose(qkv_weight[0])],
        [(COLUMNS, HALF), (UNIT, HALF)],
        [pltpu.SemaphoreType.DMA((2,))],
    )
    moved = [lax.ppermute(half, AXES, edges) for edges in MAIN]
    turned = [lax.ppermute(turn, AXES, edges) for edges in TURN]
    (outgoing,) = whole_call(
        stale_kernel, [stale_kv[0, 0]], [(2 * 4 * 2, LOCAL, 2 * PART)], [pltpu.SemaphoreType.DMA]
    )
    kv = lax.all_to_all(outgoing, ("xl", "yh", "core"), split_axis=0, concat_axis=0, tiled=True)
    kv = kv.reshape(TOKENS // 2, 2 * PART)
    (own,) = whole_call(join_kernel, [*moved, *turned], [(BLOCK, HALF)])
    up1, down1 = lax.ppermute(own, AXES, UP), lax.ppermute(own, AXES, DOWN)
    up1, entering, kv = lax.optimization_barrier((up1, hidden[0], kv))
    kv_other = lax.ppermute(kv, AXES, ACROSS)
    x = lax.all_gather(entering, ("xl", "core"), axis=0, tiled=True)
    up2, down2 = lax.ppermute(up1, AXES, UP), lax.ppermute(down1, AXES, DOWN)
    down2, x = lax.optimization_barrier((down2, x))
    up3, down3 = lax.ppermute(up2, AXES, UP), lax.ppermute(down2, AXES, DOWN)
    up4 = lax.ppermute(up3[:COLUMNS], AXES, UP)
    down4 = lax.ppermute(down3[COLUMNS:], AXES, DOWN)
    both = (0, 1)
    early = ((0, both), (-1, both), (1, both), (-2, both), (2, both)), [own, up1, down1, up2, down2]
    late = ((-3, both), (3, both), (4, (0,)), (4, (1,))), [up3, down3, up4, down4]
    rows = place(early[0], "first", early[1])
    _, weight = place(late[0], "last", late[1], [rows])
    x = jnp.transpose(x.reshape(GROUP, MEMBERS, PART), (1, 0, 2))
    near = lax.dynamic_index_in_dim(x, member, 0, keepdims=False)
    cross = lax.dynamic_index_in_dim(x, member + 1 - 2 * index["core"], 0, keepdims=False)
    far = lax.dynamic_slice_in_dim(x, 2 - index["xl"] * 2, 2, 0)

    row = lax.dynamic_index_in_dim(modulation[0, 0], timestep[0], 0, keepdims=False)
    mod = row[: 2 * D].reshape(2, D)
    gate = lax.dynamic_slice_in_dim(row, 2 * D + member * PART, PART, 0).reshape(1, PART)

    lane = jnp.arange(GROUP, dtype=jnp.int32)
    source = lane // LOCAL
    patch = (source // 2 * 4 + index["yh"]) * 2 + source % 2
    blocks = patch * (LOCAL // ROWS) + lane % LOCAL // ROWS
    positions = (patch_order[index["xh"] * (TOKENS // 2 // ROWS) + blocks] * ROWS + lane % ROWS).astype(jnp.float32)
    halfway = HDIM // 2
    inverse = jnp.exp(-math.log(10000.0) * jnp.arange(halfway, dtype=jnp.float32) / halfway)
    angles = positions[:, None] * inverse[None, :]
    cosine, sine = jnp.cos(angles), jnp.sin(angles)
    cosine = jnp.concatenate([cosine, cosine], axis=1)
    sine = jnp.concatenate([-sine, sine], axis=1)

    fresh = jnp.zeros((GROUP, 2 * PART), jnp.bfloat16)
    for tick in range(SECTIONS):
        state, fresh = run_block(tick, near, cross, far, weight, kv, kv_other, mod, gate, cosine, sine, blocks[:, None], fresh)
        if tick == 0:
            moved, state = lax.optimization_barrier((early[1] + late[1], state))
            weight = place(early[0] + late[0], "rest", moved, [weight])
        if tick == SECTIONS - 2:
            state, weight = lax.optimization_barrier((state, weight))
            weight = renew(weight)
        if tick + 1 < SECTIONS:
            far = lax.ppermute(state, AXES, onward(tick, 1, 0))
            near = lax.ppermute(state, AXES, onward(tick, 0, 0))
            cross = lax.ppermute(state, AXES, onward(tick, 0, 1))
            far = lax.all_gather(far, "core", axis=0, tiled=False)

    ends = lax.all_gather(state, ("xl", "core"), axis=0, tiled=False)
    finals = lax.dynamic_slice_in_dim(ends, member * LOCAL, LOCAL, 1)
    finals = jnp.transpose(finals, (1, 0, 2)).reshape(SECTIONS, LOCAL // SECTIONS, 2, D // 2)
    finals = jnp.transpose(finals, (0, 2, 1, 3)).reshape(SECTIONS * 2, LOCAL // SECTIONS, D // 2)
    spread = lax.all_to_all(finals, ("section", "cfg"), split_axis=0, concat_axis=0, tiled=True)
    kept = lax.all_gather(fresh, ("xl", "core"), axis=0, tiled=False)
    kept = lax.dynamic_slice_in_dim(kept, member * LOCAL, LOCAL, 1)
    kept = jnp.transpose(kept.reshape(MEMBERS, LOCAL, 2, PART), (1, 2, 0, 3)).reshape(LOCAL, 2 * D)
    spread, kept = lax.optimization_barrier((spread, kept))
    uncond = spread[2 * SECTIONS - 2].astype(jnp.float32)
    conditioned = spread[2 * SECTIONS - 1].astype(jnp.float32)
    guided = (uncond + guide_weight * (conditioned - uncond)).astype(jnp.bfloat16)
    return guided, kept[None, None]


def solution(mesh):
    fine = Mesh(mesh.devices.reshape(SIZES), AXES)
    patch = ("xh", "xl", "yh", "core")
    return jax.shard_map(
        body,
        mesh=fine,
        in_specs=(
            P("cfg", patch, None),
            P(),
            P(),
            P("section", "cfg", None, None),
            P("section", None, patch),
            P("section", "cfg", patch, None),
        ),
        out_specs=(P((*patch, "section"), "cfg"), P("section", "cfg", patch, None)),
        check_vma=False,
    )
```

```python
import functools
import math

import jax
import jax.numpy as jnp
import numpy as np
from jax import lax
from jax.experimental import pallas as pl
from jax.experimental.pallas import tpu as pltpu
from jax.sharding import Mesh, PartitionSpec as P

HEADS = 12
HDIM = 128
ROWS = 8
D = HEADS * HDIM
TOKENS = 512
SECTIONS = 8
MEMBERS = 4
PART = D // MEMBERS
LOCAL = 16
GROUP = LOCAL * MEMBERS
UNIT = 48
UNITS = 3
COLUMNS = UNIT * UNITS
HALF = D // 2
BLOCK = 2 * COLUMNS

guide_weight = 3.5
norm_eps = 1e-06

AXES = ("xh", "xl", "yh", "core", "section", "cfg")
SIZES = (2, 2, 4, 2, 8, 2)


def route(step):
    def number(x, y, core, section):
        return (((x * 4 + y // 2) * 2 + core) * 8 + section) * 2 + y % 2

    return [
        (number(x, y, core, s), number(*step(x, y, core), s))
        for x in range(4)
        for y in range(8)
        for core in range(2)
        for s in range(SECTIONS)
    ]


def member_at(x, y, core, row):
    return (((y // 2 * 2 + core) * COLUMNS + row) // PART - x) % 4


def spread(copy, row):
    def step(x, y, core):
        member = member_at(x, y, core, row(y, core))
        return (copy(core) * 2 + member // 2, y, member % 2)

    return route(step)


def cut(y, core):
    if (y // 2, core) == (1, 0):
        return 1, 2 * UNIT, 0
    if (y // 2, core) == (2, 1):
        return 1, 0, UNIT
    return 0, 0, 0


MAIN = [spread(lambda core, k=k: core ^ k, lambda y, core: cut(y, core)[2]) for k in range(2)]
TURN = [spread(lambda core, k=k: k, lambda y, core: cut(y, core)[1]) for k in range(2)]
_CUTS = {n for n in range(512) if cut(n // 16 // 2 % 4 * 2 + n % 2, n // 16 % 2)[0]}
TURN = [[edge for edge in edges if edge[0] in _CUTS] for edges in TURN]
UP = route(lambda x, y, core: (x, (y + 1 - 2 * core) % 8, core))
DOWN = route(lambda x, y, core: (x, (y - 1 + 2 * core) % 8, core))
ACROSS = [(i, (i + 256) % 512) for i in range(512)]


def place_of(x, y, core, section):
    return (((x * 4 + y // 2) * 2 + core) * 8 + section) * 2 + y % 2


PLANE = [(x, y, core) for x in range(4) for y in range(8) for core in range(2)]
LAST = SECTIONS - 1


def onward(tick, flip, turn):
    return [
        (place_of(x, y, core, section), place_of(x ^ flip, y, core ^ turn, section + 1))
        for section in range(tick % 4, LAST, 4)
        for x, y, core in PLANE
    ]


def nt_dot(a, b):
    return lax.dot_general(a, b, (((1,), (1,)), ((), ())), preferred_element_type=jnp.float32)


def block_kernel(tick, near_ref, cross_ref, far_ref, w_ref, kv_ref, other_ref, mod_ref, gate_ref, cos_ref, sin_ref, block_ref, old_ref, state_ref, fresh_ref):
    active = lax.axis_index("section") == tick
    member = lax.axis_index("xl") * 2 + lax.axis_index("core")

    @pl.when(jnp.logical_not(active))
    def _():
        fresh_ref[...] = old_ref[...]

    @pl.when(active)
    def _():
        active_block(member, near_ref, cross_ref, far_ref, w_ref, kv_ref, other_ref, mod_ref, gate_ref, cos_ref, sin_ref, block_ref, state_ref, fresh_ref)


def active_block(member, near_ref, cross_ref, far_ref, w_ref, kv_ref, other_ref, mod_ref, gate_ref, cos_ref, sin_ref, block_ref, state_ref, fresh_ref):
    near, cross = near_ref[...].astype(jnp.float32), cross_ref[...].astype(jnp.float32)
    first = member % 2 == 0
    near = [jnp.where(first, near, cross), jnp.where(first, cross, near)]
    far = [far_ref[core].astype(jnp.float32) for core in range(2)]
    low = member < 2
    xs = [jnp.where(low, near[core], far[core]) for core in range(2)]
    xs += [jnp.where(low, far[core], near[core]) for core in range(2)]
    center = sum(jnp.sum(x, axis=-1, keepdims=True) for x in xs) / D
    xs = [x - center for x in xs]
    spread = sum(jnp.sum(x * x, axis=-1, keepdims=True) for x in xs) / D
    inv = lax.rsqrt(spread + norm_eps)
    normed = jnp.concatenate(
        [
            (
                xs[i] * inv * (1.0 + mod_ref[1:2, i * PART : (i + 1) * PART])
                + mod_ref[0:1, i * PART : (i + 1) * PART]
            ).astype(jnp.bfloat16)
            for i in range(MEMBERS)
        ],
        axis=1,
    )
    projected = jnp.dot(normed, w_ref[...], preferred_element_type=jnp.float32).astype(jnp.bfloat16)
    row_block = block_ref[...]
    stale_mask = lax.broadcasted_iota(jnp.int32, (GROUP, TOKENS // 2), 1) // ROWS == row_block
    own_mask = (
        lax.broadcasted_iota(jnp.int32, (GROUP, GROUP), 0) // ROWS
        == lax.broadcasted_iota(jnp.int32, (GROUP, GROUP), 1) // ROWS
    )
    cosine, sine = cos_ref[...], sin_ref[...]

    def turned(values):
        values = values.astype(jnp.float32)
        values = values * lax.rsqrt(jnp.mean(values * values, axis=-1, keepdims=True) + norm_eps)
        return (values * cosine + pltpu.roll(values, HDIM // 2, 1) * sine).astype(jnp.bfloat16)

    heads = range(PART // HDIM)
    cols = [slice(h * HDIM, (h + 1) * HDIM) for h in heads]
    vcols = [slice(PART + h * HDIM, PART + (h + 1) * HDIM) for h in heads]
    scale = 1.0 / math.sqrt(HDIM)
    query = [turned(projected[:, cols[h]]) for h in heads]
    key = [turned(projected[:, vcols[h]]) for h in heads]
    value = [projected[:, 2 * PART + h * HDIM : 2 * PART + (h + 1) * HDIM] for h in heads]
    scores = [nt_dot(query[h], kv_ref[:, cols[h]]) for h in heads]
    other_scores = [nt_dot(query[h], other_ref[:, cols[h]]) for h in heads]
    own_scores = [nt_dot(query[h], key[h]) for h in heads]
    weights = [jnp.where(stale_mask, 0.0, jnp.exp(scores[h] * scale)) for h in heads]
    others = [jnp.exp(other_scores[h] * scale) for h in heads]
    own = [jnp.where(own_mask, jnp.exp(own_scores[h] * scale), 0.0) for h in heads]
    total = [
        jnp.sum(weights[h] + others[h], axis=-1, keepdims=True) + jnp.sum(own[h], axis=-1, keepdims=True)
        for h in heads
    ]
    attended = [
        jnp.dot(weights[h].astype(jnp.bfloat16), kv_ref[:, vcols[h]], preferred_element_type=jnp.float32)
        + jnp.dot(others[h].astype(jnp.bfloat16), other_ref[:, vcols[h]], preferred_element_type=jnp.float32)
        + jnp.dot(own[h].astype(jnp.bfloat16), value[h], preferred_element_type=jnp.float32)
        for h in heads
    ]
    for h in heads:
        state = near_ref[:, cols[h]].astype(jnp.float32) + gate_ref[0:1, cols[h]] * (attended[h] / total[h])
        state_ref[:, cols[h]] = state.astype(jnp.bfloat16)
        fresh_ref[:, cols[h]] = key[h]
        fresh_ref[:, vcols[h]] = value[h]


def run_block(tick, near, cross, far, weight, kv, other, mod, gate, cosine, sine, blocks, old):
    vmem = pl.BlockSpec(memory_space=pltpu.VMEM)
    weight = pltpu.with_memory_space_constraint(weight, pltpu.VMEM)
    return pl.pallas_call(
        functools.partial(block_kernel, tick),
        out_shape=(
            jax.ShapeDtypeStruct((GROUP, PART), jnp.bfloat16),
            jax.ShapeDtypeStruct((GROUP, 2 * PART), jnp.bfloat16),
        ),
        in_specs=[vmem] * 12,
        out_specs=(vmem, vmem),
        compiler_params=pltpu.CompilerParams(vmem_limit_bytes=8 * 1024 * 1024),
        name="block_step",
    )(near, cross, far, weight, kv, other, mod, gate, cosine, sine, blocks, old)


def seat():
    y = lax.axis_index("yh") * 2 + lax.axis_index("cfg")
    core = lax.axis_index("core")
    later = jnp.minimum(lax.axis_index("section"), 1)
    return lax.axis_index("xl") * 2 + core, lax.axis_index("xh"), core, y, later


def half_kernel(columns_ref, half_ref, turn_ref, sems):
    _, _, core, y, _ = seat()
    first = (1 - core) * (2 * UNIT)
    col = pl.ds(pl.multiple_of(y % 2 * HALF, 128), HALF)
    whole = pltpu.make_async_copy(columns_ref.at[:, col], half_ref, sems.at[0])
    turn = pltpu.make_async_copy(
        columns_ref.at[pl.ds(pl.multiple_of(first, 16), UNIT), col], turn_ref, sems.at[1]
    )
    whole.start()
    turn.start()
    whole.wait()
    turn.wait()


def stale_kernel(stale_ref, out_ref):
    for slot in range(2 * 4 * 2):
        m = slot // 8 * 2 + slot % 2
        out_ref[slot, :, :PART] = stale_ref[:, m * PART : (m + 1) * PART]
        out_ref[slot, :, PART:] = stale_ref[:, D + m * PART : D + (m + 1) * PART]


def join_kernel(first_ref, second_ref, turn0_ref, turn1_ref, own_ref):
    _, half, _, y, _ = seat()

    def pick(one, two):
        return jnp.where(half == 0, one[...], two[...])

    own_ref[:COLUMNS, :] = pick(first_ref, second_ref)
    own_ref[COLUMNS:, :] = pick(second_ref, first_ref)

    @pl.when(y // 2 == 1)
    def _():
        own_ref[2 * UNIT : COLUMNS, :] = pick(turn0_ref, turn1_ref)

    @pl.when(y // 2 == 2)
    def _():
        own_ref[COLUMNS : COLUMNS + UNIT, :] = pick(turn0_ref, turn1_ref)


def place_kernel(sources, kind, *refs):
    blocks, refs = refs[: len(sources)], refs[len(sources) :]
    rows = refs[{"first": 0, "last": 1, "rest": 2}[kind]]
    sem = refs[-1]
    member, _, core, y, later = seat()
    sign = 1 - 2 * core

    def home(unit):
        third = unit // 8
        part = (COLUMNS * 8 * ((third - member + 4) % 4) + PART * third) // D
        return part * PART + unit % 8 * UNIT

    @pl.when(later == (1 if kind == "rest" else 0))
    def _():
        copies = []
        for (source, parts), ref in zip(sources, blocks):
            at = (y + sign * source + 8) % 8
            col = pl.ds(pl.multiple_of(at % 2 * HALF, 128), HALF)
            for n, part in enumerate(parts):
                for j in range(UNITS):
                    row = pl.multiple_of(home((at // 2 * 2 + part) * UNITS + j), 16)
                    copy = pltpu.make_async_copy(
                        ref.at[pl.ds(n * COLUMNS + j * UNIT, UNIT)], rows.at[pl.ds(row, UNIT), col], sem
                    )
                    copy.start()
                    copies.append(copy)
        for copy in copies:
            copy.wait()
        if kind != "first":
            out_ref = refs[2 if kind == "last" else 1]
            for c in range(0, D, HDIM):
                out_ref[c : c + HDIM, :] = jnp.transpose(rows[:, c : c + HDIM])


def place(sources, kind, blocks, held=()):
    any_space = pl.BlockSpec(memory_space=pl.ANY)
    vmem = pl.BlockSpec(memory_space=pltpu.VMEM)
    whole = jax.ShapeDtypeStruct((3 * PART, D), jnp.bfloat16)
    turned = jax.ShapeDtypeStruct((D, 3 * PART), jnp.bfloat16)
    scratch = [pltpu.SemaphoreType.DMA]
    if kind == "rest":
        scratch = [pltpu.VMEM((3 * PART, D), jnp.bfloat16), *scratch]
    return pl.pallas_call(
        functools.partial(place_kernel, sources, kind),
        out_shape={"first": whole, "last": (whole, turned), "rest": turned}[kind],
        in_specs=[any_space] * len(blocks) + [vmem] * len(held),
        out_specs=(vmem, vmem) if kind == "last" else vmem,
        input_output_aliases={len(blocks): 0} if held else {},
        scratch_shapes=scratch,
        compiler_params=pltpu.CompilerParams(vmem_limit_bytes=12 * 1024 * 1024),
        name="place_" + kind,
    )(*blocks, *held)


def renew_kernel(weight_ref, out_ref, sem):
    copy = pltpu.make_async_copy(weight_ref, out_ref, sem)
    copy.start()
    copy.wait()


def renew(weight):
    vmem = pl.BlockSpec(memory_space=pltpu.VMEM)
    return pl.pallas_call(
        renew_kernel,
        out_shape=jax.ShapeDtypeStruct(weight.shape, weight.dtype),
        in_specs=[vmem],
        out_specs=vmem,
        scratch_shapes=[pltpu.SemaphoreType.DMA],
        compiler_params=pltpu.CompilerParams(vmem_limit_bytes=8 * 1024 * 1024),
        name="renew_weight",
    )(pltpu.with_memory_space_constraint(weight, pltpu.VMEM))


def whole_call(kernel, arrays, outs, sems=()):
    vmem = pl.BlockSpec(memory_space=pltpu.VMEM)
    held = pl.BlockSpec(memory_space=pl.ANY) if sems else vmem
    return pl.pallas_call(
        kernel,
        out_shape=[jax.ShapeDtypeStruct(shape, jnp.bfloat16) for shape in outs],
        in_specs=[held] * len(arrays),
        out_specs=[vmem] * len(outs),
        scratch_shapes=list(sems),
        compiler_params=pltpu.CompilerParams(vmem_limit_bytes=8 * 1024 * 1024),
        name=kernel.__name__,
    )(*arrays)


def body(hidden, timestep, patch_order, modulation, qkv_weight, stale_kv):
    index = {a: lax.axis_index(a) for a in AXES}
    section = index["section"]
    member = index["xl"] * 2 + index["core"]

    half, turn = whole_call(
        half_kernel,
        [jnp.transpose(qkv_weight[0])],
        [(COLUMNS, HALF), (UNIT, HALF)],
        [pltpu.SemaphoreType.DMA((2,))],
    )
    moved = [lax.ppermute(half, AXES, edges) for edges in MAIN]
    turned = [lax.ppermute(turn, AXES, edges) for edges in TURN]
    (outgoing,) = whole_call(
        stale_kernel, [stale_kv[0, 0]], [(2 * 4 * 2, LOCAL, 2 * PART)]
    )
    kv = lax.all_to_all(outgoing, ("xl", "yh", "core"), split_axis=0, concat_axis=0, tiled=True)
    kv = kv.reshape(TOKENS // 2, 2 * PART)
    (own,) = whole_call(join_kernel, [*moved, *turned], [(BLOCK, HALF)])
    up1, down1 = lax.ppermute(own, AXES, UP), lax.ppermute(own, AXES, DOWN)
    up1, entering, kv = lax.optimization_barrier((up1, hidden[0], kv))
    kv_other = lax.ppermute(kv, AXES, ACROSS)
    x = lax.all_gather(entering, ("xl", "core"), axis=0, tiled=True)
    up2, down2 = lax.ppermute(up1, AXES, UP), lax.ppermute(down1, AXES, DOWN)
    down2, x = lax.optimization_barrier((down2, x))
    up3, down3 = lax.ppermute(up2, AXES, UP), lax.ppermute(down2, AXES, DOWN)
    up4 = lax.ppermute(up3[:COLUMNS], AXES, UP)
    down4 = lax.ppermute(down3[COLUMNS:], AXES, DOWN)
    both = (0, 1)
    early = ((0, both), (-1, both), (1, both), (-2, both), (2, both)), [own, up1, down1, up2, down2]
    late = ((-3, both), (3, both), (4, (0,)), (4, (1,))), [up3, down3, up4, down4]
    rows = place(early[0], "first", early[1])
    _, weight = place(late[0], "last", late[1], [rows])
    x = jnp.transpose(x.reshape(GROUP, MEMBERS, PART), (1, 0, 2))
    near = lax.dynamic_index_in_dim(x, member, 0, keepdims=False)
    cross = lax.dynamic_index_in_dim(x, member + 1 - 2 * index["core"], 0, keepdims=False)
    far = lax.dynamic_slice_in_dim(x, 2 - index["xl"] * 2, 2, 0)

    row = lax.dynamic_index_in_dim(modulation[0, 0], timestep[0], 0, keepdims=False)
    mod = row[: 2 * D].reshape(2, D)
    gate = lax.dynamic_slice_in_dim(row, 2 * D + member * PART, PART, 0).reshape(1, PART)

    lane = jnp.arange(GROUP, dtype=jnp.int32)
    source = lane // LOCAL
    patch = (source // 2 * 4 + index["yh"]) * 2 + source % 2
    blocks = patch * (LOCAL // ROWS) + lane % LOCAL // ROWS
    positions = (patch_order[index["xh"] * (TOKENS // 2 // ROWS) + blocks] * ROWS + lane % ROWS).astype(jnp.float32)
    halfway = HDIM // 2
    inverse = jnp.exp(-math.log(10000.0) * jnp.arange(halfway, dtype=jnp.float32) / halfway)
    angles = positions[:, None] * inverse[None, :]
    cosine, sine = jnp.cos(angles), jnp.sin(angles)
    cosine = jnp.concatenate([cosine, cosine], axis=1)
    sine = jnp.concatenate([-sine, sine], axis=1)

    fresh = jnp.zeros((GROUP, 2 * PART), jnp.bfloat16)
    for tick in range(SECTIONS):
        state, fresh = run_block(tick, near, cross, far, weight, kv, kv_other, mod, gate, cosine, sine, blocks[:, None], fresh)
        if tick == 0:
            moved, state = lax.optimization_barrier((early[1] + late[1], state))
            weight = place(early[0] + late[0], "rest", moved, [weight])
        if tick == SECTIONS - 2:
            state, weight = lax.optimization_barrier((state, weight))
            weight = renew(weight)
        if tick + 1 < SECTIONS:
            far = lax.ppermute(state, AXES, onward(tick, 1, 0))
            near = lax.ppermute(state, AXES, onward(tick, 0, 0))
            cross = lax.ppermute(state, AXES, onward(tick, 0, 1))
            far = lax.all_gather(far, "core", axis=0, tiled=False)

    ends = lax.all_gather(state, ("xl", "core"), axis=0, tiled=False)
    finals = lax.dynamic_slice_in_dim(ends, member * LOCAL, LOCAL, 1)
    finals = jnp.transpose(finals, (1, 0, 2)).reshape(SECTIONS, LOCAL // SECTIONS, 2, D // 2)
    finals = jnp.transpose(finals, (0, 2, 1, 3)).reshape(SECTIONS * 2, LOCAL // SECTIONS, D // 2)
    spread = lax.all_to_all(finals, ("section", "cfg"), split_axis=0, concat_axis=0, tiled=True)
    kept = lax.all_gather(fresh, ("xl", "core"), axis=0, tiled=False)
    kept = lax.dynamic_slice_in_dim(kept, member * LOCAL, LOCAL, 1)
    kept = jnp.transpose(kept.reshape(MEMBERS, LOCAL, 2, PART), (1, 2, 0, 3)).reshape(LOCAL, 2 * D)
    spread, kept = lax.optimization_barrier((spread, kept))
    uncond = spread[2 * SECTIONS - 2].astype(jnp.float32)
    conditioned = spread[2 * SECTIONS - 1].astype(jnp.float32)
    guided = (uncond + guide_weight * (conditioned - uncond)).astype(jnp.bfloat16)
    return guided, kept[None, None]


def solution(mesh):
    fine = Mesh(mesh.devices.reshape(SIZES), AXES)
    patch = ("xh", "xl", "yh", "core")
    return jax.shard_map(
        body,
        mesh=fine,
        in_specs=(
            P("cfg", patch, None),
            P(),
            P(),
            P("section", "cfg", None, None),
            P("section", None, patch),
            P("section", "cfg", patch, None),
        ),
        out_specs=(P((*patch, "section"), "cfg"), P("section", "cfg", patch, None)),
        check_vma=False,
    )
```

```python
import functools
import math

import jax
import jax.numpy as jnp
import numpy as np
from jax import lax
from jax.experimental import pallas as pl
from jax.experimental.pallas import tpu as pltpu
from jax.sharding import Mesh, PartitionSpec as P

HEADS = 12
HDIM = 128
ROWS = 8
D = HEADS * HDIM
TOKENS = 512
SECTIONS = 8
MEMBERS = 4
PART = D // MEMBERS
LOCAL = 16
GROUP = LOCAL * MEMBERS
UNIT = 48
UNITS = 3
COLUMNS = UNIT * UNITS
HALF = D // 2
BLOCK = 2 * COLUMNS

guide_weight = 3.5
norm_eps = 1e-06

AXES = ("xh", "xl", "yh", "core", "section", "cfg")
SIZES = (2, 2, 4, 2, 8, 2)


def route(step):
    def number(x, y, core, section):
        return (((x * 4 + y // 2) * 2 + core) * 8 + section) * 2 + y % 2

    return [
        (number(x, y, core, s), number(*step(x, y, core), s))
        for x in range(4)
        for y in range(8)
        for core in range(2)
        for s in range(SECTIONS)
    ]


def member_at(x, y, core, row):
    return (((y // 2 * 2 + core) * COLUMNS + row) // PART - x) % 4


def spread(copy, row):
    def step(x, y, core):
        member = member_at(x, y, core, row(y, core))
        return (copy(core) * 2 + member // 2, y, member % 2)

    return route(step)


def cut(y, core):
    if (y // 2, core) == (1, 0):
        return 1, 2 * UNIT, 0
    if (y // 2, core) == (2, 1):
        return 1, 0, UNIT
    return 0, 0, 0


MAIN = [spread(lambda core, k=k: core ^ k, lambda y, core: cut(y, core)[2]) for k in range(2)]
TURN = [spread(lambda core, k=k: k, lambda y, core: cut(y, core)[1]) for k in range(2)]
_CUTS = {n for n in range(512) if cut(n // 16 // 2 % 4 * 2 + n % 2, n // 16 % 2)[0]}
TURN = [[edge for edge in edges if edge[0] in _CUTS] for edges in TURN]
UP = route(lambda x, y, core: (x, (y + 1 - 2 * core) % 8, core))
DOWN = route(lambda x, y, core: (x, (y - 1 + 2 * core) % 8, core))
ACROSS = [(i, (i + 256) % 512) for i in range(512)]


def place_of(x, y, core, section):
    return (((x * 4 + y // 2) * 2 + core) * 8 + section) * 2 + y % 2


PLANE = [(x, y, core) for x in range(4) for y in range(8) for core in range(2)]
LAST = SECTIONS - 1


def onward(tick, flip, turn):
    return [
        (place_of(x, y, core, section), place_of(x ^ flip, y, core ^ turn, section + 1))
        for section in range(tick % 4, LAST, 4)
        for x, y, core in PLANE
    ]


def nt_dot(a, b):
    return lax.dot_general(a, b, (((1,), (1,)), ((), ())), preferred_element_type=jnp.float32)


def block_kernel(tick, near_ref, cross_ref, far_ref, w_ref, kv_ref, other_ref, mod_ref, gate_ref, cos_ref, sin_ref, block_ref, old_ref, state_ref, fresh_ref):
    active = lax.axis_index("section") == tick
    member = lax.axis_index("xl") * 2 + lax.axis_index("core")

    @pl.when(jnp.logical_not(active))
    def _():
        fresh_ref[...] = old_ref[...]

    @pl.when(active)
    def _():
        active_block(member, near_ref, cross_ref, far_ref, w_ref, kv_ref, other_ref, mod_ref, gate_ref, cos_ref, sin_ref, block_ref, state_ref, fresh_ref)


def active_block(member, near_ref, cross_ref, far_ref, w_ref, kv_ref, other_ref, mod_ref, gate_ref, cos_ref, sin_ref, block_ref, state_ref, fresh_ref):
    near, cross = near_ref[...].astype(jnp.float32), cross_ref[...].astype(jnp.float32)
    first = member % 2 == 0
    near = [jnp.where(first, near, cross), jnp.where(first, cross, near)]
    far = [far_ref[core].astype(jnp.float32) for core in range(2)]
    low = member < 2
    xs = [jnp.where(low, near[core], far[core]) for core in range(2)]
    xs += [jnp.where(low, far[core], near[core]) for core in range(2)]
    center = sum(jnp.sum(x, axis=-1, keepdims=True) for x in xs) / D
    xs = [x - center for x in xs]
    spread = sum(jnp.sum(x * x, axis=-1, keepdims=True) for x in xs) / D
    inv = lax.rsqrt(spread + norm_eps)
    normed = jnp.concatenate(
        [
            (
                xs[i] * inv * (1.0 + mod_ref[1:2, i * PART : (i + 1) * PART])
                + mod_ref[0:1, i * PART : (i + 1) * PART]
            ).astype(jnp.bfloat16)
            for i in range(MEMBERS)
        ],
        axis=1,
    )
    projected = jnp.dot(normed, w_ref[...], preferred_element_type=jnp.float32).astype(jnp.bfloat16)
    row_block = block_ref[...]
    stale_mask = lax.broadcasted_iota(jnp.int32, (GROUP, TOKENS // 2), 1) // ROWS == row_block
    own_mask = (
        lax.broadcasted_iota(jnp.int32, (GROUP, GROUP), 0) // ROWS
        == lax.broadcasted_iota(jnp.int32, (GROUP, GROUP), 1) // ROWS
    )
    cosine, sine = cos_ref[...], sin_ref[...]

    def turned(values):
        values = values.astype(jnp.float32)
        values = values * lax.rsqrt(jnp.mean(values * values, axis=-1, keepdims=True) + norm_eps)
        return (values * cosine + pltpu.roll(values, HDIM // 2, 1) * sine).astype(jnp.bfloat16)

    heads = range(PART // HDIM)
    cols = [slice(h * HDIM, (h + 1) * HDIM) for h in heads]
    vcols = [slice(PART + h * HDIM, PART + (h + 1) * HDIM) for h in heads]
    scale = math.log2(math.e) / math.sqrt(HDIM)
    query = [turned(projected[:, cols[h]]) for h in heads]
    key = [turned(projected[:, vcols[h]]) for h in heads]
    value = [projected[:, 2 * PART + h * HDIM : 2 * PART + (h + 1) * HDIM] for h in heads]
    scores = [nt_dot(query[h], kv_ref[:, cols[h]]) for h in heads]
    other_scores = [nt_dot(query[h], other_ref[:, cols[h]]) for h in heads]
    own_scores = [nt_dot(query[h], key[h]) for h in heads]
    weights = [jnp.where(stale_mask, 0.0, jnp.exp2(scores[h] * scale)) for h in heads]
    others = [jnp.exp2(other_scores[h] * scale) for h in heads]
    own = [jnp.where(own_mask, jnp.exp2(own_scores[h] * scale), 0.0) for h in heads]
    total = [
        jnp.sum(weights[h] + others[h], axis=-1, keepdims=True) + jnp.sum(own[h], axis=-1, keepdims=True)
        for h in heads
    ]
    attended = [
        jnp.dot(weights[h].astype(jnp.bfloat16), kv_ref[:, vcols[h]], preferred_element_type=jnp.float32)
        + jnp.dot(others[h].astype(jnp.bfloat16), other_ref[:, vcols[h]], preferred_element_type=jnp.float32)
        + jnp.dot(own[h].astype(jnp.bfloat16), value[h], preferred_element_type=jnp.float32)
        for h in heads
    ]
    for h in heads:
        state = near_ref[:, cols[h]].astype(jnp.float32) + gate_ref[0:1, cols[h]] * (attended[h] / total[h])
        state_ref[:, cols[h]] = state.astype(jnp.bfloat16)
        fresh_ref[:, cols[h]] = key[h]
        fresh_ref[:, vcols[h]] = value[h]


def run_block(tick, near, cross, far, weight, kv, other, mod, gate, cosine, sine, blocks, old):
    vmem = pl.BlockSpec(memory_space=pltpu.VMEM)
    weight = pltpu.with_memory_space_constraint(weight, pltpu.VMEM)
    return pl.pallas_call(
        functools.partial(block_kernel, tick),
        out_shape=(
            jax.ShapeDtypeStruct((GROUP, PART), jnp.bfloat16),
            jax.ShapeDtypeStruct((GROUP, 2 * PART), jnp.bfloat16),
        ),
        in_specs=[vmem] * 12,
        out_specs=(vmem, vmem),
        compiler_params=pltpu.CompilerParams(vmem_limit_bytes=8 * 1024 * 1024),
        name="block_step",
    )(near, cross, far, weight, kv, other, mod, gate, cosine, sine, blocks, old)


def seat():
    y = lax.axis_index("yh") * 2 + lax.axis_index("cfg")
    core = lax.axis_index("core")
    later = jnp.minimum(lax.axis_index("section"), 1)
    return lax.axis_index("xl") * 2 + core, lax.axis_index("xh"), core, y, later


def half_kernel(columns_ref, half_ref, turn_ref, sems):
    _, _, core, y, _ = seat()
    first = (1 - core) * (2 * UNIT)
    col = pl.ds(pl.multiple_of(y % 2 * HALF, 128), HALF)
    whole = pltpu.make_async_copy(columns_ref.at[:, col], half_ref, sems.at[0])
    turn = pltpu.make_async_copy(
        columns_ref.at[pl.ds(pl.multiple_of(first, 16), UNIT), col], turn_ref, sems.at[1]
    )
    whole.start()
    turn.start()
    whole.wait()
    turn.wait()


def stale_kernel(stale_ref, out_ref, sem):
    copies = []
    for slot in range(2 * 4 * 2):
        m = slot // 8 * 2 + slot % 2
        for part in range(2):
            copies.append(
                pltpu.make_async_copy(
                    stale_ref.at[:, part * D + m * PART : part * D + (m + 1) * PART],
                    out_ref.at[slot, :, part * PART : (part + 1) * PART],
                    sem,
                )
            )
            copies[-1].start()
    for copy in copies:
        copy.wait()


def join_kernel(first_ref, second_ref, turn0_ref, turn1_ref, own_ref):
    _, half, _, y, _ = seat()

    def pick(one, two):
        return jnp.where(half == 0, one[...], two[...])

    own_ref[:COLUMNS, :] = pick(first_ref, second_ref)
    own_ref[COLUMNS:, :] = pick(second_ref, first_ref)

    @pl.when(y // 2 == 1)
    def _():
        own_ref[2 * UNIT : COLUMNS, :] = pick(turn0_ref, turn1_ref)

    @pl.when(y // 2 == 2)
    def _():
        own_ref[COLUMNS : COLUMNS + UNIT, :] = pick(turn0_ref, turn1_ref)


def place_kernel(sources, kind, *refs):
    blocks, refs = refs[: len(sources)], refs[len(sources) :]
    rows = refs[{"first": 0, "last": 1, "rest": 2}[kind]]
    sem = refs[-1]
    member, _, core, y, later = seat()
    sign = 1 - 2 * core

    def home(unit):
        third = unit // 8
        part = (COLUMNS * 8 * ((third - member + 4) % 4) + PART * third) // D
        return part * PART + unit % 8 * UNIT

    @pl.when(later == (1 if kind == "rest" else 0))
    def _():
        copies = []
        for (source, parts), ref in zip(sources, blocks):
            at = (y + sign * source + 8) % 8
            col = pl.ds(pl.multiple_of(at % 2 * HALF, 128), HALF)
            for n, part in enumerate(parts):
                for j in range(UNITS):
                    row = pl.multiple_of(home((at // 2 * 2 + part) * UNITS + j), 16)
                    copy = pltpu.make_async_copy(
                        ref.at[pl.ds(n * COLUMNS + j * UNIT, UNIT)], rows.at[pl.ds(row, UNIT), col], sem
                    )
                    copy.start()
                    copies.append(copy)
        for copy in copies:
            copy.wait()
        if kind != "first":
            out_ref = refs[2 if kind == "last" else 1]
            for c in range(0, D, HDIM):
                out_ref[c : c + HDIM, :] = jnp.transpose(rows[:, c : c + HDIM])


def place(sources, kind, blocks, held=()):
    any_space = pl.BlockSpec(memory_space=pl.ANY)
    vmem = pl.BlockSpec(memory_space=pltpu.VMEM)
    whole = jax.ShapeDtypeStruct((3 * PART, D), jnp.bfloat16)
    turned = jax.ShapeDtypeStruct((D, 3 * PART), jnp.bfloat16)
    scratch = [pltpu.SemaphoreType.DMA]
    if kind == "rest":
        scratch = [pltpu.VMEM((3 * PART, D), jnp.bfloat16), *scratch]
    return pl.pallas_call(
        functools.partial(place_kernel, sources, kind),
        out_shape={"first": whole, "last": (whole, turned), "rest": turned}[kind],
        in_specs=[any_space] * len(blocks) + [vmem] * len(held),
        out_specs=(vmem, vmem) if kind == "last" else vmem,
        input_output_aliases={len(blocks): 0} if held else {},
        scratch_shapes=scratch,
        compiler_params=pltpu.CompilerParams(vmem_limit_bytes=12 * 1024 * 1024),
        name="place_" + kind,
    )(*blocks, *held)


def renew_kernel(weight_ref, out_ref, sem):
    copy = pltpu.make_async_copy(weight_ref, out_ref, sem)
    copy.start()
    copy.wait()


def renew(weight):
    vmem = pl.BlockSpec(memory_space=pltpu.VMEM)
    return pl.pallas_call(
        renew_kernel,
        out_shape=jax.ShapeDtypeStruct(weight.shape, weight.dtype),
        in_specs=[vmem],
        out_specs=vmem,
        scratch_shapes=[pltpu.SemaphoreType.DMA],
        compiler_params=pltpu.CompilerParams(vmem_limit_bytes=8 * 1024 * 1024),
        name="renew_weight",
    )(pltpu.with_memory_space_constraint(weight, pltpu.VMEM))


def whole_call(kernel, arrays, outs, sems=()):
    vmem = pl.BlockSpec(memory_space=pltpu.VMEM)
    held = pl.BlockSpec(memory_space=pl.ANY) if sems else vmem
    return pl.pallas_call(
        kernel,
        out_shape=[jax.ShapeDtypeStruct(shape, jnp.bfloat16) for shape in outs],
        in_specs=[held] * len(arrays),
        out_specs=[vmem] * len(outs),
        scratch_shapes=list(sems),
        compiler_params=pltpu.CompilerParams(vmem_limit_bytes=8 * 1024 * 1024),
        name=kernel.__name__,
    )(*arrays)


def body(hidden, timestep, patch_order, modulation, qkv_weight, stale_kv):
    index = {a: lax.axis_index(a) for a in AXES}
    section = index["section"]
    member = index["xl"] * 2 + index["core"]

    half, turn = whole_call(
        half_kernel,
        [jnp.transpose(qkv_weight[0])],
        [(COLUMNS, HALF), (UNIT, HALF)],
        [pltpu.SemaphoreType.DMA((2,))],
    )
    moved = [lax.ppermute(half, AXES, edges) for edges in MAIN]
    turned = [lax.ppermute(turn, AXES, edges) for edges in TURN]
    (outgoing,) = whole_call(
        stale_kernel, [stale_kv[0, 0]], [(2 * 4 * 2, LOCAL, 2 * PART)], [pltpu.SemaphoreType.DMA]
    )
    kv = lax.all_to_all(outgoing, ("xl", "yh", "core"), split_axis=0, concat_axis=0, tiled=True)
    kv = kv.reshape(TOKENS // 2, 2 * PART)
    (own,) = whole_call(join_kernel, [*moved, *turned], [(BLOCK, HALF)])
    up1, down1 = lax.ppermute(own, AXES, UP), lax.ppermute(own, AXES, DOWN)
    up1, entering, kv = lax.optimization_barrier((up1, hidden[0], kv))
    kv_other = lax.ppermute(kv, AXES, ACROSS)
    x = lax.all_gather(entering, ("xl", "core"), axis=0, tiled=True)
    up2, down2 = lax.ppermute(up1, AXES, UP), lax.ppermute(down1, AXES, DOWN)
    down2, x = lax.optimization_barrier((down2, x))
    up3, down3 = lax.ppermute(up2, AXES, UP), lax.ppermute(down2, AXES, DOWN)
    up4 = lax.ppermute(up3[:COLUMNS], AXES, UP)
    down4 = lax.ppermute(down3[COLUMNS:], AXES, DOWN)
    both = (0, 1)
    early = ((0, both), (-1, both), (1, both), (-2, both), (2, both)), [own, up1, down1, up2, down2]
    late = ((-3, both), (3, both), (4, (0,)), (4, (1,))), [up3, down3, up4, down4]
    rows = place(early[0], "first", early[1])
    _, weight = place(late[0], "last", late[1], [rows])
    x = jnp.transpose(x.reshape(GROUP, MEMBERS, PART), (1, 0, 2))
    near = lax.dynamic_index_in_dim(x, member, 0, keepdims=False)
    cross = lax.dynamic_index_in_dim(x, member + 1 - 2 * index["core"], 0, keepdims=False)
    far = lax.dynamic_slice_in_dim(x, 2 - index["xl"] * 2, 2, 0)

    row = lax.dynamic_index_in_dim(modulation[0, 0], timestep[0], 0, keepdims=False)
    mod = row[: 2 * D].reshape(2, D)
    gate = lax.dynamic_slice_in_dim(row, 2 * D + member * PART, PART, 0).reshape(1, PART)

    lane = jnp.arange(GROUP, dtype=jnp.int32)
    source = lane // LOCAL
    patch = (source // 2 * 4 + index["yh"]) * 2 + source % 2
    blocks = patch * (LOCAL // ROWS) + lane % LOCAL // ROWS
    positions = (patch_order[index["xh"] * (TOKENS // 2 // ROWS) + blocks] * ROWS + lane % ROWS).astype(jnp.float32)
    halfway = HDIM // 2
    inverse = jnp.exp(-math.log(10000.0) * jnp.arange(halfway, dtype=jnp.float32) / halfway)
    angles = positions[:, None] * inverse[None, :]
    cosine, sine = jnp.cos(angles), jnp.sin(angles)
    cosine = jnp.concatenate([cosine, cosine], axis=1)
    sine = jnp.concatenate([-sine, sine], axis=1)

    fresh = jnp.zeros((GROUP, 2 * PART), jnp.bfloat16)
    for tick in range(SECTIONS):
        state, fresh = run_block(tick, near, cross, far, weight, kv, kv_other, mod, gate, cosine, sine, blocks[:, None], fresh)
        if tick == 0:
            moved, state = lax.optimization_barrier((early[1] + late[1], state))
            weight = place(early[0] + late[0], "rest", moved, [weight])
        if tick == SECTIONS - 2:
            state, weight = lax.optimization_barrier((state, weight))
            weight = renew(weight)
        if tick + 1 < SECTIONS:
            far = lax.ppermute(state, AXES, onward(tick, 1, 0))
            near = lax.ppermute(state, AXES, onward(tick, 0, 0))
            cross = lax.ppermute(state, AXES, onward(tick, 0, 1))
            far = lax.all_gather(far, "core", axis=0, tiled=False)

    ends = lax.all_gather(state, ("xl", "core"), axis=0, tiled=False)
    finals = lax.dynamic_slice_in_dim(ends, member * LOCAL, LOCAL, 1)
    finals = jnp.transpose(finals, (1, 0, 2)).reshape(SECTIONS, LOCAL // SECTIONS, 2, D // 2)
    finals = jnp.transpose(finals, (0, 2, 1, 3)).reshape(SECTIONS * 2, LOCAL // SECTIONS, D // 2)
    spread = lax.all_to_all(finals, ("section", "cfg"), split_axis=0, concat_axis=0, tiled=True)
    kept = lax.all_gather(fresh, ("xl", "core"), axis=0, tiled=False)
    kept = lax.dynamic_slice_in_dim(kept, member * LOCAL, LOCAL, 1)
    kept = jnp.transpose(kept.reshape(MEMBERS, LOCAL, 2, PART), (1, 2, 0, 3)).reshape(LOCAL, 2 * D)
    spread, kept = lax.optimization_barrier((spread, kept))
    uncond = spread[2 * SECTIONS - 2].astype(jnp.float32)
    conditioned = spread[2 * SECTIONS - 1].astype(jnp.float32)
    guided = (uncond + guide_weight * (conditioned - uncond)).astype(jnp.bfloat16)
    return guided, kept[None, None]


def solution(mesh):
    fine = Mesh(mesh.devices.reshape(SIZES), AXES)
    patch = ("xh", "xl", "yh", "core")
    return jax.shard_map(
        body,
        mesh=fine,
        in_specs=(
            P("cfg", patch, None),
            P(),
            P(),
            P("section", "cfg", None, None),
            P("section", None, patch),
            P("section", "cfg", patch, None),
        ),
        out_specs=(P((*patch, "section"), "cfg"), P("section", "cfg", patch, None)),
        check_vma=False,
    )
```
